256 devices in a mesh: dp: 128 (over x, y_lo, z, core), fsdp: 2 (over y_hi).
Axes of the slice: x: 4, y: 4 (y_hi: 2, y_lo: 2; y = y_hi * 2 + y_lo), z: 8, core: 2. Of those that a mesh axis runs over, the one named last changes fastest.
Arguments:
- img_feat: bfloat16 [8192, 1408], P('dp'), may hold values from -64 to 64
- txt_feat: bfloat16 [8192, 1408], P('dp'), may hold values from -64 to 64
- img_weight: bfloat16 [1408, 1536], P(None, 'fsdp'), may hold values from -2 to 2
- txt_weight: bfloat16 [1408, 1536], P(None, 'fsdp'), may hold values from -2 to 2
- logit_scale: float32 [1], replicated, may hold values from 30 to 60
- logit_bias: float32 [1], replicated, may hold values from -9 to -6
Outputs:
- loss: float32 [], replicated
- img_feat_grad: float32 [8192, 1408], P('dp', 'fsdp')
- txt_feat_grad: float32 [8192, 1408], P('dp', 'fsdp')
- txt_weight_grad: float32 [1408, 1536], P('dp', 'fsdp')
The draws below stay inside these ranges and needn't reach their ends.
All inputs are finite; a program needn't handle non-finite values.
Results may differ from the reference program's by a relative error of at most 0.0031.
Values may be sent and summed in bfloat16 or wider, within the bound.
A program may use at most 128 MiB of HBM per device.

```python
import math
import jax
import jax.numpy as jnp
from jax import lax

E = 1536
FEAT = 1408
B_DEV = 64
N_ROWS = 8192


cluster_count = 16


cluster_share = 0.32


content_share = 0.77


weight_noise = 0.5


def pair_content(key):
    key = jax.random.fold_in(key, 101)
    centre_key, member_key, content_key, blend_key = jax.random.split(key, 4)
    centres = jax.random.normal(centre_key, (cluster_count, FEAT), jnp.float32)
    members = jax.random.randint(member_key, (N_ROWS,), 0, cluster_count)
    content = jax.random.normal(content_key, (N_ROWS, FEAT), jnp.float32)
    blend_share = jax.random.uniform(blend_key, (N_ROWS, 1), jnp.float32, 0.2, 1.0)
    return (centres[members], content, blend_share)


def head_base(key, column_range):
    key = jax.random.fold_in(key, 202)
    base_key, column_key = jax.random.split(key)
    base_part = jax.random.normal(base_key, (FEAT, E), jnp.float32)
    column_scale = jnp.exp(jax.random.uniform(column_key, (1, E), jnp.float32, 0.0, column_range))
    return (base_part, column_scale)


def draw_img_feat(key, part):
    cluster_part, content, blend_share = pair_content(key)
    key = jax.random.fold_in(key, 3)
    noise_key, scale_key = jax.random.split(key)
    noise_weight = math.sqrt(1.0 - cluster_share ** 2 - content_share ** 2)
    noise_part = jax.random.normal(noise_key, (N_ROWS, FEAT), jnp.float32)
    row_scale = jnp.exp(jax.random.uniform(scale_key, (N_ROWS, 1), jnp.float32, 0.0, math.log(3.0)))
    mixed_rows = cluster_share * cluster_part + content_share * content + noise_weight * noise_part
    return jnp.clip(row_scale * mixed_rows, -64.0, 64.0).astype(jnp.bfloat16)


def draw_txt_feat(key, part):
    cluster_part, content, blend_share = pair_content(key)
    key = jax.random.fold_in(key, 4)
    noise_key, scale_key = jax.random.split(key)
    noise_weight = jnp.sqrt(1.0 - cluster_share ** 2 - (content_share * blend_share) ** 2)
    noise_part = jax.random.normal(noise_key, (N_ROWS, FEAT), jnp.float32)
    row_scale = jnp.exp(jax.random.uniform(scale_key, (N_ROWS, 1), jnp.float32, 0.0, math.log(3.0)))
    mixed_rows = cluster_share * cluster_part + content_share * blend_share * content + noise_weight * noise_part
    return jnp.clip(row_scale * mixed_rows, -64.0, 64.0).astype(jnp.bfloat16)


def draw_img_weight(key, part):
    base_part, column_scale = head_base(key, math.log(3.0))
    key = jax.random.fold_in(key, 5)
    own_part = jax.random.normal(key, (FEAT, E), jnp.float32)
    mixed_head = column_scale * (base_part + weight_noise * own_part) / math.sqrt(1.25 * FEAT)
    return jnp.clip(mixed_head, -2.0, 2.0).astype(jnp.bfloat16)


def draw_txt_weight(key, part):
    base_part, column_scale = head_base(key, math.log(3.0))
    key = jax.random.fold_in(key, 6)
    own_part = jax.random.normal(key, (FEAT, E), jnp.float32)
    mixed_head = column_scale * (base_part + weight_noise * own_part) / math.sqrt(1.25 * FEAT)
    return jnp.clip(mixed_head, -2.0, 2.0).astype(jnp.bfloat16)


def setup_inputs(seed: int = 0) -> dict:
    keys = jax.random.split(jax.random.key(seed), 7)
    img_feat = draw_img_feat(jax.random.fold_in(keys[6], 71), 0)
    txt_feat = draw_txt_feat(jax.random.fold_in(keys[6], 71), 0)
    img_weight = draw_img_weight(jax.random.fold_in(keys[6], 71), 0)
    txt_weight = draw_txt_weight(jax.random.fold_in(keys[6], 71), 0)
    logit_scale = jnp.clip(jnp.exp(jax.random.uniform(keys[4], (1,), jnp.float32, math.log(30.0), math.log(60.0))), 30.0, 60.0)
    logit_bias = jnp.clip(jax.random.uniform(keys[5], (1,), jnp.float32, -9.0, -6.0), -9.0, -6.0)
    return {"img_feat": img_feat, "txt_feat": txt_feat, "img_weight": img_weight, "txt_weight": txt_weight, "logit_scale": logit_scale, "logit_bias": logit_bias}


EPS = 1e-06

def embed_rows(features, weight):
    projected = jnp.dot(features, weight, preferred_element_type=jnp.float32)
    norm_rows = jnp.sqrt(lax.optimization_barrier(jnp.sum(projected * projected, axis=1, keepdims=True)) + EPS)
    return (norm_rows, projected / norm_rows)

def directional(queries, key_units, scale_value, bias_value):
    block_count = queries.shape[0] // B_DEV

    def one_block(block_id):
        row_start = (block_id * B_DEV).astype(jnp.int32)
        query_rows = lax.dynamic_slice_in_dim(queries, row_start, B_DEV, 0)
        logits = scale_value * jnp.dot(query_rows, key_units.T, preferred_element_type=jnp.float32) + bias_value
        row_ids = row_start + jnp.arange(B_DEV, dtype=jnp.int32)[:, None]
        col_ids = jnp.arange(key_units.shape[0], dtype=jnp.int32)[None, :]
        label_sign = jnp.where(row_ids == col_ids, 1.0, -1.0).astype(jnp.float32)
        summed = jnp.sum(jax.nn.softplus(-label_sign * logits))
        slope = (-label_sign * jax.nn.sigmoid(-label_sign * logits) * scale_value).astype(jnp.bfloat16)
        grad_part = jnp.dot(slope, key_units, preferred_element_type=jnp.float32)
        return (grad_part, summed)
    grads, totals = lax.map(one_block, jnp.arange(block_count, dtype=jnp.int32))
    return (grads.reshape(-1, key_units.shape[1]), jnp.sum(totals))

def backward_norm(unit_grad, unit_rows, norm_rows):
    inner = lax.optimization_barrier(jnp.sum(unit_rows * unit_grad, axis=1, keepdims=True))
    return ((unit_grad - unit_rows * inner) / norm_rows).astype(jnp.bfloat16)

def reference(img_feat, txt_feat, img_weight, txt_weight, logit_scale, logit_bias):
    scale_value = logit_scale[0]
    bias_value = logit_bias[0]
    img_norm, img_unit = embed_rows(img_feat, img_weight)
    txt_norm, txt_unit = embed_rows(txt_feat, txt_weight)
    img_emb = img_unit.astype(jnp.bfloat16)
    txt_emb = txt_unit.astype(jnp.bfloat16)
    img_grad, summed = directional(img_emb, txt_emb, scale_value, bias_value)
    txt_grad, unused = directional(txt_emb, img_emb, scale_value, bias_value)
    loss_value = summed / N_ROWS
    img_proj_grad = backward_norm(img_grad, img_unit, img_norm)
    txt_proj_grad = backward_norm(txt_grad, txt_unit, txt_norm)
    img_feat_grad = jnp.dot(img_proj_grad, img_weight.T, preferred_element_type=jnp.float32)
    txt_feat_grad = jnp.dot(txt_proj_grad, txt_weight.T, preferred_element_type=jnp.float32)
    txt_weight_grad = jnp.dot(txt_feat.T, txt_proj_grad, preferred_element_type=jnp.float32)
    return (loss_value, img_feat_grad, txt_feat_grad, txt_weight_grad)
```

```python
import jax
import jax.numpy as jnp
from jax import lax
from jax.experimental import pallas as pl
from jax.experimental.pallas import tpu as pltpu
from jax.sharding import PartitionSpec as P

EPS = 1e-06
MESH = pl.DeviceIdType.MESH
BF = jnp.bfloat16
F32 = jnp.float32
R = 32
E = 1536
H = 768
FEAT = 1408
FH = 704
N_SEM = 112


def dot_nt(a, b):
    return lax.dot_general(a, b, (((1,), (1,)), ((), ())), preferred_element_type=F32)


def dot_tn(a, b):
    return lax.dot_general(a, b, (((0,), (0,)), ((), ())), preferred_element_type=F32)


def kernel(
    scale_ref, bias_ref, img_feat, txt_feat, img_w_hbm, txt_w_hbm,
    loss_out, img_out, txt_out, wg_out,
    w_img, w_txt, proj, proj_rcv, full, norms,
    txt_all, img_all, slope_s, feat_win,
    a_send, a_rcv, a_own, a2_send, a2_rcv,
    b_send, b_rcv, b_own, b2_send, b2_rcv,
    ci_send, ci_rcv, pi_own, zp_send, zp_rcv, zm_send, zm_rcv,
    pgf, pg64, pgx, fg_send, fg_rcv,
    wg, cw_send, cw_rcv, y_send, y_rcv, s2, zw_rcv,
    lx, ly, lc, lz, loss_v,
    ssem, rsem, wsem,
):
    dp = lax.axis_index("dp")
    yh = lax.axis_index("fsdp")
    c = lax.rem(dp, 2)
    z = lax.rem(dp // 2, 8)
    yl = lax.rem(dp // 16, 2)
    x = dp // 32
    y = yh * 2 + yl

    def dev(x_, y_, z_, c_):
        return {"dp": ((x_ * 2 + lax.rem(y_, 2)) * 8 + z_) * 2 + c_, "fsdp": y_ // 2}

    def dx(k):
        return dev(lax.rem(x + k, 4), y, z, c)

    def dy(k):
        return dev(x, lax.rem(y + k, 4), z, c)

    def dz(k):
        return dev(x, y, lax.rem(z + k, 8), c)

    other = dev(x, y, z, 1 - c)
    fs_partner = dy(2)
    yl_partner = dev(x, yh * 2 + (1 - yl), z, c)

    counter = [0]

    def copy(src, dst, target):
        i = counter[0]
        counter[0] += 1
        cp = pltpu.make_async_remote_copy(
            src_ref=src, dst_ref=dst, send_sem=ssem.at[i], recv_sem=rsem.at[i],
            device_id=target, device_id_type=MESH,
        )
        cp.start()
        sent.append(cp)
        return cp

    sent = []

    load_txt = pltpu.make_async_copy(txt_w_hbm, w_txt, wsem.at[0])
    load_img = pltpu.make_async_copy(img_w_hbm, w_img, wsem.at[1])
    load_txt.start()
    load_img.start()

    barrier = pltpu.get_barrier_semaphore()
    partners = [dx(k) for k in (1, 2, 3)] + [dy(k) for k in (1, 2, 3)]
    partners += [dz(k) for k in range(1, 8)] + [other]
    for p in partners:
        pl.semaphore_signal(barrier, inc=1, device_id=p, device_id_type=MESH)

    mine = pl.ds(pl.multiple_of(yh * R, R), R)
    theirs = pl.ds(pl.multiple_of((1 - yh) * R, R), R)
    my_cols = pl.ds(pl.multiple_of(yh * H, 128), H)
    their_cols = pl.ds(pl.multiple_of((1 - yh) * H, 128), H)

    load_txt.wait()
    proj[1] = jnp.dot(txt_feat[...], w_txt[...], preferred_element_type=F32)
    pl.semaphore_wait(barrier, len(partners))
    swap_txt = copy(proj.at[1, theirs], proj_rcv.at[1], fs_partner)
    load_img.wait()
    proj[0] = jnp.dot(img_feat[...], w_img[...], preferred_element_type=F32)
    swap_img = copy(proj.at[0, theirs], proj_rcv.at[0], fs_partner)

    def window(x_):
        return pl.ds(pl.multiple_of(256 * x_ + 128 * (x_ // 2), 128), 512)

    feat_win[0] = txt_feat[:, window(x)]

    def embed(m):
        own = proj[m, mine, :]
        got = proj_rcv[m]
        total = jnp.sum(own * own, axis=1, keepdims=True) + jnp.sum(got * got, axis=1, keepdims=True)
        norm = jnp.sqrt(total + EPS)
        norms[m] = jnp.broadcast_to(norm, (R, 128))
        full[m, :, my_cols] = own / norm
        full[m, :, their_cols] = got / norm
        return full[m].astype(BF)

    A = pl.ds(0, H)
    B = pl.ds(H, H)

    swap_txt.wait_recv()
    txt_all[0, 0] = embed(1)
    ax = {}
    ay = {}
    bx = {}
    by = {}
    for k in (1, 3, 2):
        ax[k] = copy(txt_all.at[0, 0, :, A], txt_all.at[4 - k, 0, :, A], dx(k))
        by[k] = copy(txt_all.at[0, 0, :, B], txt_all.at[0, 4 - k, :, B], dy(k))
    swap_img.wait_recv()
    img_all[0, 0] = embed(0)
    zp = {}
    zm = {}
    cf = {}
    zp[1] = copy(img_all.at[0, 0], img_all.at[0, 7], dz(1))
    zm[1] = copy(img_all.at[0, 0], img_all.at[0, 1], dz(7))
    cf[0] = copy(img_all.at[0, 0], img_all.at[1, 0], other)
    for k in (1, 3, 2):
        ay[0, k] = copy(txt_all.at[0, 0, :, A], txt_all.at[0, 4 - k, :, A], dy(k))
        bx[0, k] = copy(txt_all.at[0, 0, :, B], txt_all.at[4 - k, 0, :, B], dx(k))

    def second(k):
        slot = 4 - k
        ax[k].wait_recv()
        for j in (1, 3, 2):
            ay[slot, j] = copy(txt_all.at[slot, 0, :, A], txt_all.at[slot, 4 - j, :, A], dy(j))
        by[k].wait_recv()
        for j in (1, 3, 2):
            bx[slot, j] = copy(txt_all.at[0, slot, :, B], txt_all.at[4 - j, slot, :, B], dx(j))

    second(1)
    second(3)
    for step in (1, 2):
        zp[step].wait_recv()
        zp[step + 1] = copy(img_all.at[0, 8 - step], img_all.at[0, 7 - step], dz(1))
        cf[8 - step] = copy(img_all.at[0, 8 - step], img_all.at[1, 8 - step], other)
        zm[step].wait_recv()
        zm[step + 1] = copy(img_all.at[0, step], img_all.at[0, step + 1], dz(7))
        cf[step] = copy(img_all.at[0, step], img_all.at[1, step], other)
        if step == 1:
            second(2)
    zp[3].wait_recv()
    zp[4] = copy(img_all.at[0, 5, :, A], img_all.at[0, 4, :, A], dz(1))
    cf[5] = copy(img_all.at[0, 5], img_all.at[1, 5], other)
    zm[3].wait_recv()
    zm[4] = copy(img_all.at[0, 3, :, B], img_all.at[0, 4, :, B], dz(7))
    cf[3] = copy(img_all.at[0, 3], img_all.at[1, 3], other)
    zp[4].wait_recv()
    zm[4].wait_recv()
    cf[4] = copy(img_all.at[0, 4], img_all.at[1, 4], other)
    for s in range(4):
        for j in (1, 2, 3):
            ay[s, j].wait_recv()
            bx[s, j].wait_recv()
    for s in range(8):
        cf[s].wait_recv()

    fw = [copy(txt_feat.at[:, window(lax.rem(x + k, 4))], feat_win.at[4 - k], dx(k)) for k in (1, 2, 3)]

    scale = scale_ref[0]
    bias = bias_ref[0]
    txt_rows = txt_all[...].reshape(16 * R, E)
    loss_v[...] = jnp.zeros_like(loss_v)

    def tile(i, carry):
        row0 = pl.multiple_of(i * 4, 4)
        rows = img_all[i // 2, pl.ds(pl.multiple_of((i % 2) * 4, 4), 4)].reshape(4 * R, E)
        logits = scale * dot_nt(rows, txt_rows) + bias
        ri = lax.broadcasted_iota(jnp.int32, logits.shape, 0) + i * (4 * R)
        ci = lax.broadcasted_iota(jnp.int32, logits.shape, 1)
        label = jnp.where((ri == ci) & (ri < R), 1.0, -1.0).astype(F32)
        v = -label * logits
        t = jnp.exp(-jnp.abs(v))
        loss_v[...] += jnp.sum((jnp.maximum(v, 0.0) + jnp.log1p(t)).reshape(16, 8, 16 * R), axis=0)
        sig = jnp.where(v >= 0, 1.0, t) / (1.0 + t)
        slope_s[pl.ds(pl.multiple_of(i * 4 * R, 4 * R), 4 * R), :] = (-label * sig * scale).astype(BF)
        return carry

    lax.fori_loop(0, 4, tile, 0)

    img_rows = img_all[...].reshape(16 * R, E)
    sa = {}
    for k in (1, 3, 2, 0):
        g = dot_tn(slope_s[:, k * 128:(k + 1) * 128], img_rows)
        ga = g[:, :H].reshape(4, R, H)
        gb = g[:, H:].reshape(4, R, H)
        if k:
            a_send[k - 1] = ga.astype(BF)
            sa[k] = copy(a_send.at[k - 1], a_rcv.at[3 - k], dx(k))
        else:
            a_own[...] = ga
        b_own[k] = gb[0]
        for j in (1, 2, 3):
            b_send[j - 1, k] = gb[j].astype(BF)
    sb = {}
    for j in (1, 3, 2):
        sb[j] = copy(b_send.at[j - 1], b_rcv.at[3 - j], dy(j))

    ci_send[...] = jnp.dot(
        slope_s[8 * R:, :], txt_rows, preferred_element_type=F32
    ).astype(BF).reshape(8, R, E)
    ci_copy = copy(ci_send, ci_rcv, other)
    pi_own[...] = jnp.dot(slope_s[:8 * R, :], txt_rows, preferred_element_type=F32).reshape(8, R, E)

    part = jnp.sum(loss_v[...])
    lx[0] = jnp.full((8, 128), part, F32)
    lxc = [copy(lx.at[0], lx.at[4 - k], dx(k)) for k in (1, 2, 3)]

    ci_copy.wait_recv()
    pi_own[...] += ci_rcv[...].astype(F32)

    zp_send[0] = pi_own[4].astype(BF)
    rzp = [copy(zp_send.at[0, :, A], zp_rcv.at[0, :, A], dz(1))]
    rzm = [copy(zp_send.at[0, :, B], zm_rcv.at[0, :, B], dz(7))]

    def ring(step):
        rzp[step - 1].wait_recv()
        rzm[step - 1].wait_recv()
        if step == 1:
            zp_send[1, :, A] = (pi_own[3, :, A] + zp_rcv[0, :, A].astype(F32)).astype(BF)
            zp_send[1, :, B] = pi_own[3, :, B].astype(BF)
            zm_send[1, :, B] = (pi_own[5, :, B] + zm_rcv[0, :, B].astype(F32)).astype(BF)
            zm_send[1, :, A] = pi_own[5, :, A].astype(BF)
        else:
            zp_send[step] = (pi_own[4 - step] + zp_rcv[step - 1].astype(F32)).astype(BF)
            zm_send[step] = (pi_own[4 + step] + zm_rcv[step - 1].astype(F32)).astype(BF)
        rzp.append(copy(zp_send.at[step], zp_rcv.at[step], dz(1)))
        rzm.append(copy(zm_send.at[step], zm_rcv.at[step], dz(7)))

    ring(1)

    for k in (1, 2, 3):
        sa[k].wait_recv()
    ga = a_own[...] + a_rcv[0].astype(F32) + a_rcv[1].astype(F32) + a_rcv[2].astype(F32)
    a2_send[...] = ga[1:].astype(BF)
    a2 = [copy(a2_send.at[k - 1], a2_rcv.at[3 - k], dy(k)) for k in (1, 2, 3)]
    for k in (1, 2, 3):
        sb[k].wait_recv()
    gb = b_own[...] + b_rcv[0].astype(F32) + b_rcv[1].astype(F32) + b_rcv[2].astype(F32)
    b2_send[...] = gb[1:].astype(BF)
    b2 = [copy(b2_send.at[k - 1], b2_rcv.at[3 - k], dx(k)) for k in (1, 2, 3)]
    ga0 = ga[0]
    gb0 = gb[0]

    for cp in lxc:
        cp.wait_recv()
    ly[0] = (lx[0] + lx[2]) + (lx[1] + lx[3])
    lyc = [copy(ly.at[0], ly.at[4 - k], dy(k)) for k in (1, 2, 3)]

    ring(2)

    for cp in a2:
        cp.wait_recv()
    for cp in b2:
        cp.wait_recv()
    ga0 = ga0 + a2_rcv[0].astype(F32) + a2_rcv[1].astype(F32) + a2_rcv[2].astype(F32)
    gb0 = gb0 + b2_rcv[0].astype(F32) + b2_rcv[1].astype(F32) + b2_rcv[2].astype(F32)

    def back(m, ga, gb):
        ua = full[m, :, A]
        ub = full[m, :, B]
        inner = jnp.sum(ua * ga, axis=1, keepdims=True) + jnp.sum(ub * gb, axis=1, keepdims=True)
        norm = norms[m, :, 0:1]
        pgf[m, :, A] = ((ga - ua * inner) / norm).astype(BF)
        pgf[m, :, B] = ((gb - ub * inner) / norm).astype(BF)
        cp = copy(pgf.at[m, :, their_cols], pg64.at[m, mine], fs_partner)
        pg64[m, mine, :] = pgf[m, :, my_cols]
        return cp

    pg_txt = back(1, ga0, gb0)
    ring(3)
    pg_txt.wait_recv()
    pgx[0] = pg64[1]
    px = [copy(pg64.at[1], pgx.at[4 - k], dx(k)) for k in (1, 3, 2)]

    my_feat = pl.ds(pl.multiple_of(yh * FH, 16), FH)
    their_feat = pl.ds(pl.multiple_of((1 - yh) * FH, 16), FH)

    def feature_terms(m, w):
        fg_send[m] = dot_nt(pg64[m], w[their_feat, :])
        cp = copy(fg_send.at[m], fg_rcv.at[m], fs_partner)
        return cp

    fg_txt = feature_terms(1, w_txt)
    txt_out[...] = dot_nt(pg64[1], w_txt[my_feat, :])

    for cp in lyc:
        cp.wait_recv()
    lc[0] = (ly[0] + ly[2]) + (ly[1] + ly[3])
    lcc = copy(lc.at[0], lc.at[1], other)

    for cp in fw:
        cp.wait_recv()
    for cp in px:
        cp.wait_recv()
    wg[0:512, :] = dot_tn(feat_win[...].reshape(4 * 64, 512), pgx[...].reshape(4 * 64, H))
    wg[512:528, :] = jnp.zeros((16, H), F32)
    start = 352 * x - (256 * x + 128 * (x // 2))

    def rows16(k, core):
        first = start + 22 * k + 11 * core
        low = first // 8
        block = wg[pl.ds(pl.multiple_of(low * 8, 8), 24), :]
        return pltpu.roll(block, 24 - (first - low * 8), 0)[:16]

    def cut(k, carry):
        cw_send[k] = rows16(k, 1 - c).astype(BF)
        return carry

    lax.fori_loop(0, 16, cut, 0)
    cw = copy(cw_send, cw_rcv, other)

    rzp[3].wait_recv()
    rzm[3].wait_recv()
    gi = pi_own[0] + zp_rcv[3].astype(F32) + zm_rcv[3].astype(F32)
    pg_img = back(0, gi[:, :H], gi[:, H:])

    cw.wait_recv()

    def add_core(k, carry):
        kk = (1 - yl) * 8 + k
        y_send[k] = (
            rows16(kk, c) + cw_rcv[kk].astype(F32)
        ).astype(BF)
        return carry

    lax.fori_loop(0, 8, add_core, 0)
    yw = copy(y_send, y_rcv, yl_partner)

    lcc.wait_recv()
    lz[0] = lc[0] + lc[1]
    lzc = [copy(lz.at[0], lz.at[8 - k], dz(k)) for k in range(1, 8)]

    pg_img.wait_recv()
    fg_img = feature_terms(0, w_img)
    img_out[...] = dot_nt(pg64[0], w_img[my_feat, :])

    yw.wait_recv()

    def add_y(k, carry):
        kk = yl * 8 + k
        s2[k] = (
            rows16(kk, c) + cw_rcv[kk].astype(F32) + y_rcv[k].astype(F32)
        ).astype(BF)
        return carry

    lax.fori_loop(0, 8, add_y, 0)
    zw = [copy(s2.at[lax.rem(z + k, 8)], zw_rcv.at[7 - k], dz(k)) for k in (1, 7, 2, 6, 3, 5, 4)]
    own_w = (
        rows16(yl * 8 + z, c) + cw_rcv[yl * 8 + z].astype(F32) + y_rcv[z].astype(F32)
    )

    fg_txt.wait_recv()
    txt_out[...] += fg_rcv[1]
    for cp in lzc:
        cp.wait_recv()
    total = ((lz[0] + lz[4]) + (lz[2] + lz[6])) + ((lz[1] + lz[5]) + (lz[3] + lz[7]))
    loss_out[...] = total / 8192.0
    for cp in zw:
        cp.wait_recv()
    for k in range(7):
        own_w = own_w + zw_rcv[k].astype(F32)
    wg_out[...] = own_w[:11, :]
    fg_img.wait_recv()
    img_out[...] += fg_rcv[0]
    for cp in sent:
        cp.wait_send()


def body(img_feat, txt_feat, img_weight, txt_weight, logit_scale, logit_bias):
    vm = pl.BlockSpec(memory_space=pltpu.VMEM)
    sm = pl.BlockSpec(memory_space=pltpu.SMEM)
    hbm = pl.BlockSpec(memory_space=pl.ANY)
    V = pltpu.VMEM
    loss, img_grad, txt_grad, w_grad = pl.pallas_call(
        kernel,
        out_shape=(
            jax.ShapeDtypeStruct((8, 128), F32),
            jax.ShapeDtypeStruct((64, FH), F32),
            jax.ShapeDtypeStruct((64, FH), F32),
            jax.ShapeDtypeStruct((11, H), F32),
        ),
        in_specs=[sm, sm, vm, vm, hbm, hbm],
        out_specs=(vm, vm, vm, vm),
        scratch_shapes=[
            V((FEAT, H), BF), V((FEAT, H), BF),
            V((2, 64, H), F32), V((2, R, H), F32), V((2, R, E), F32), V((2, R, 128), F32),
            V((4, 4, R, E), BF), V((2, 8, R, E), BF), V((16 * R, 16 * R), BF), V((4, 64, 512), BF),
            V((3, 4, R, H), BF), V((3, 4, R, H), BF), V((4, R, H), F32), V((3, R, H), BF), V((3, R, H), BF),
            V((3, 4, R, H), BF), V((3, 4, R, H), BF), V((4, R, H), F32), V((3, R, H), BF), V((3, R, H), BF),
            V((8, R, E), BF), V((8, R, E), BF), V((8, R, E), F32),
            V((4, R, E), BF), V((4, R, E), BF), V((4, R, E), BF), V((4, R, E), BF),
            V((2, R, E), BF), V((2, 64, H), BF), V((4, 64, H), BF), V((2, 64, FH), F32), V((2, 64, FH), F32),
            V((528, H), F32), V((16, 16, H), BF), V((16, 16, H), BF), V((8, 16, H), BF), V((8, 16, H), BF),
            V((8, 16, H), BF), V((7, 16, H), BF),
            V((4, 8, 128), F32), V((4, 8, 128), F32), V((2, 8, 128), F32), V((8, 8, 128), F32),
            V((8, 16 * R), F32),
            pltpu.SemaphoreType.DMA((N_SEM,)),
            pltpu.SemaphoreType.DMA((N_SEM,)),
            pltpu.SemaphoreType.DMA((2,)),
        ],
        compiler_params=pltpu.CompilerParams(
            collective_id=0, has_side_effects=True, vmem_limit_bytes=56 * 1024 * 1024
        ),
        name="fused",
    )(logit_scale, logit_bias, img_feat, txt_feat, img_weight, txt_weight)
    return loss[0, 0], img_grad, txt_grad, w_grad


def solution(mesh):
    placed = (P("dp", None), P("dp", None), P(None, "fsdp"), P(None, "fsdp"), P(), P())
    return jax.shard_map(
        body,
        mesh=mesh,
        in_specs=placed,
        out_specs=(P(), P("dp", "fsdp"), P("dp", "fsdp"), P("dp", "fsdp")),
        check_vma=False,
    )
```

```python
import jax
import jax.numpy as jnp
from jax import lax
from jax.experimental import pallas as pl
from jax.experimental.pallas import tpu as pltpu
from jax.sharding import PartitionSpec as P

EPS = 1e-06
MESH = pl.DeviceIdType.MESH
BF = jnp.bfloat16
F32 = jnp.float32
R = 32
E = 1536
H = 768
FEAT = 1408
FH = 704
N_SEM = 160
ORDER = [(2, 2), (2, 1), (2, 3), (1, 2), (3, 2), (1, 1), (1, 3), (3, 1), (3, 3), (2, 0), (0, 2), (1, 0), (3, 0), (0, 1), (0, 3)]


def dot_nt(a, b):
    return lax.dot_general(a, b, (((1,), (1,)), ((), ())), preferred_element_type=F32)


def dot_tn(a, b):
    return lax.dot_general(a, b, (((0,), (0,)), ((), ())), preferred_element_type=F32)


def kernel(
    scale_ref, bias_ref, img_f_hbm, txt_f_hbm, img_w_hbm, txt_w_hbm,
    loss_out, img_out, txt_out, wg_out,
    img_feat, txt_feat, w_img, w_txt, proj, proj_rcv, full, norms,
    txt_all, img_all, slope_s, feat_win,
    a_send, a_rcv, a_own, a2_send, a2_rcv,
    b_send, b_rcv, b_own, b2_send, b2_rcv,
    ci_send, ci_rcv, pi_own, zp_send, zp_rcv, zm_send, zm_rcv,
    pgf, pg64, pg_plane, fi_send, fi_rcv, ft_send, ft_rcv,
    wg, cw_send, cw_rcv, s2, zw_rcv,
    lx, ly, lc, lz, logit_s,
    ssem, rsem, wsem,
):
    dp = lax.axis_index("dp")
    yh = lax.axis_index("fsdp")
    c = lax.rem(dp, 2)
    z = lax.rem(dp // 2, 8)
    yl = lax.rem(dp // 16, 2)
    x = dp // 32
    y = yh * 2 + yl

    def dev(x_, y_, z_, c_):
        return {"dp": ((x_ * 2 + lax.rem(y_, 2)) * 8 + z_) * 2 + c_, "fsdp": y_ // 2}

    def dx(k):
        return dev(lax.rem(x + k, 4), y, z, c)

    def dy(k):
        return dev(x, lax.rem(y + k, 4), z, c)

    def dz(k):
        return dev(x, y, lax.rem(z + k, 8), c)

    other = dev(x, y, z, 1 - c)
    fs_partner = dy(2)

    def dxy(i, j):
        return dev(lax.rem(x + i, 4), lax.rem(y + j, 4), z, c)

    def dyz(k):
        return dev(x, yh * 2 + (1 - yl), lax.rem(z + k, 8), c)

    counter = [0]

    def copy(src, dst, target):
        i = counter[0]
        counter[0] += 1
        cp = pltpu.make_async_remote_copy(
            src_ref=src, dst_ref=dst, send_sem=ssem.at[i], recv_sem=rsem.at[i],
            device_id=target, device_id_type=MESH,
        )
        cp.start()
        sent.append(cp)
        return cp

    sent = []

    loads = [
        pltpu.make_async_copy(img_f_hbm, img_feat, wsem.at[0]),
        pltpu.make_async_copy(img_w_hbm, w_img, wsem.at[1]),
        pltpu.make_async_copy(txt_f_hbm, txt_feat, wsem.at[2]),
        pltpu.make_async_copy(txt_w_hbm, w_txt, wsem.at[3]),
    ]
    for load in loads:
        load.start()

    barrier = pltpu.get_barrier_semaphore()
    partners = [dx(k) for k in (1, 2, 3)] + [dy(k) for k in (1, 2, 3)]
    partners += [dz(k) for k in range(1, 8)] + [other]
    partners += [dxy(i, j) for i in (1, 2, 3) for j in (1, 2, 3)]
    partners += [dyz(k) for k in range(1, 8)]
    for p in partners:
        pl.semaphore_signal(barrier, inc=1, device_id=p, device_id_type=MESH)

    mine = pl.ds(pl.multiple_of(yh * R, R), R)
    theirs = pl.ds(pl.multiple_of((1 - yh) * R, R), R)
    my_cols = pl.ds(pl.multiple_of(yh * H, 128), H)
    their_cols = pl.ds(pl.multiple_of((1 - yh) * H, 128), H)

    def window(x_):
        return pl.ds(pl.multiple_of(256 * x_ + 128 * (x_ // 2), 128), 512)

    loads[0].wait()
    loads[1].wait()
    proj[0] = jnp.dot(img_feat[...], w_img[...], preferred_element_type=F32)
    pl.semaphore_wait(barrier, len(partners))
    swap_img = copy(proj.at[0, theirs], proj_rcv.at[0], fs_partner)
    loads[2].wait()
    loads[3].wait()
    proj[1] = jnp.dot(txt_feat[...], w_txt[...], preferred_element_type=F32)
    swap_txt = copy(proj.at[1, theirs], proj_rcv.at[1], fs_partner)

    fw = []
    for i in (2, 1, 3):
        cols = window(lax.rem(x + i, 4))
        fw.append(copy(txt_feat.at[mine, cols], feat_win.at[4 - i, 0], dx(i)))
        fw.append(copy(txt_feat.at[theirs, cols], feat_win.at[4 - i, 2], dx(i)))
    for i in (2, 1, 3, 0):
        cols = window(lax.rem(x + i, 4))
        for j in (1, 3):
            fw.append(copy(txt_feat.at[mine, cols], feat_win.at[(4 - i) % 4, 4 - j], dxy(i, j)))
    feat_win[0, 0] = txt_feat[mine, window(x)]
    feat_win[0, 2] = txt_feat[theirs, window(x)]

    def embed(m):
        own = proj[m, mine, :]
        got = proj_rcv[m]
        total = jnp.sum(own * own, axis=1, keepdims=True) + jnp.sum(got * got, axis=1, keepdims=True)
        norm = jnp.sqrt(total + EPS)
        norms[m] = jnp.broadcast_to(norm, (R, 128))
        full[m, :, my_cols] = own / norm
        full[m, :, their_cols] = got / norm
        return full[m].astype(BF)

    A = pl.ds(0, H)
    B = pl.ds(H, H)

    zp = {}
    zm = {}
    cf = {}

    swap_img.wait_recv()
    img_all[0, 0] = embed(0)
    for part in (A, B):
        zp[1, part.start] = copy(img_all.at[0, 0, :, part], img_all.at[0, 7, :, part], dz(1))
        zm[1, part.start] = copy(img_all.at[0, 0, :, part], img_all.at[0, 1, :, part], dz(7))
    cf[0] = copy(img_all.at[0, 0], img_all.at[1, 0], other)
    swap_txt.wait_recv()
    txt_all[0, 0] = embed(1)
    ax = {}
    ay = {}
    bx = {}
    by = {}
    for k in (1, 3, 2):
        ax[k] = copy(txt_all.at[0, 0, :, A], txt_all.at[4 - k, 0, :, A], dx(k))
        by[k] = copy(txt_all.at[0, 0, :, B], txt_all.at[0, 4 - k, :, B], dy(k))
    for k in (1, 3, 2):
        ay[0, k] = copy(txt_all.at[0, 0, :, A], txt_all.at[0, 4 - k, :, A], dy(k))
        bx[0, k] = copy(txt_all.at[0, 0, :, B], txt_all.at[4 - k, 0, :, B], dx(k))

    def second(k):
        slot = 4 - k
        ax[k].wait_recv()
        for j in (1, 3, 2):
            ay[slot, j] = copy(txt_all.at[slot, 0, :, A], txt_all.at[slot, 4 - j, :, A], dy(j))
        by[k].wait_recv()
        for j in (1, 3, 2):
            bx[slot, j] = copy(txt_all.at[0, slot, :, B], txt_all.at[4 - j, slot, :, B], dx(j))

    def along_z(step):
        for part in (A, B):
            p = part.start
            zp[step, p].wait_recv()
            if step < 3 or p == 0:
                zp[step + 1, p] = copy(img_all.at[0, 8 - step, :, part], img_all.at[0, 7 - step, :, part], dz(1))
            zm[step, p].wait_recv()
            if step < 3 or p == H:
                zm[step + 1, p] = copy(img_all.at[0, step, :, part], img_all.at[0, step + 1, :, part], dz(7))
        cf[8 - step] = copy(img_all.at[0, 8 - step], img_all.at[1, 8 - step], other)
        cf[step] = copy(img_all.at[0, step], img_all.at[1, step], other)

    along_z(1)
    second(1)
    second(3)
    along_z(2)
    second(2)
    along_z(3)
    zp[4, 0].wait_recv()
    zm[4, H].wait_recv()
    cf[4] = copy(img_all.at[0, 4], img_all.at[1, 4], other)
    for s in range(4):
        for j in (1, 2, 3):
            ay[s, j].wait_recv()
            bx[s, j].wait_recv()
    for s in range(8):
        cf[s].wait_recv()

    scale = scale_ref[...]
    bias = bias_ref[...]
    txt_rows = txt_all[...].reshape(16 * R, E)
    img_rows = img_all[...].reshape(16 * R, E)
    for i in range(2):
        half = slice(i * 8 * R, (i + 1) * 8 * R)
        logit_s[half, :] = dot_nt(img_rows[half], txt_rows)

    def strip(i, acc, diagonal):
        rows = pl.ds(pl.multiple_of(i * R, R), R)
        v = scale * logit_s[rows, :] + bias
        if diagonal:
            ri = lax.broadcasted_iota(jnp.int32, v.shape, 0)
            ci = lax.broadcasted_iota(jnp.int32, v.shape, 1)
            v = jnp.where(ri == ci, -v, v)
        t = jnp.exp(-jnp.abs(v))
        grad = scale * (jnp.where(v >= 0, 1.0, t) / (1.0 + t))
        if diagonal:
            grad = jnp.where(ri == ci, -grad, grad)
        slope_s[rows, :] = grad.astype(BF)
        m = jnp.maximum(v, 0.0)
        prod = t[0:8]
        for j in (8, 16, 24):
            prod = prod + t[j:j + 8] * (1.0 + prod)
        return acc + jnp.log1p(prod) + ((m[0:8] + m[8:16]) + (m[16:24] + m[24:32]))

    acc = strip(0, jnp.zeros((8, 16 * R), F32), True)
    acc = lax.fori_loop(1, 16, lambda i, a: strip(i, a, False), acc, unroll=3)

    sa = {}
    sb = {}
    for k in (1, 3, 2, 0):
        g = dot_tn(slope_s[:, k * 128:(k + 1) * 128], img_rows)
        ga = g[:, :H].reshape(4, R, H)
        gb = g[:, H:].reshape(4, R, H)
        if k:
            a_send[k - 1] = ga.astype(BF)
            sa[k] = copy(a_send.at[k - 1], a_rcv.at[3 - k], dx(k))
        else:
            a_own[...] = ga
        b_own[k] = gb[0]
        b_send[:, k] = gb[1:].astype(BF)
        for j in (1, 3, 2):
            sb[j, k] = copy(b_send.at[j - 1, k], b_rcv.at[3 - j, k], dy(j))

    ci_send[...] = jnp.dot(
        slope_s[8 * R:, :], txt_rows, preferred_element_type=F32
    ).astype(BF).reshape(8, R, E)
    ci_copy = copy(ci_send, ci_rcv, other)
    pi_own[...] = jnp.dot(slope_s[:8 * R, :], txt_rows, preferred_element_type=F32).reshape(8, R, E)

    part = jnp.sum(acc)
    lx[0] = jnp.full((8, 128), part, F32)
    lxc = [copy(lx.at[0], lx.at[4 - k], dx(k)) for k in (1, 2, 3)]

    ci_copy.wait_recv()
    pi_own[...] += ci_rcv[...].astype(F32)

    zp_send[0] = pi_own[4].astype(BF)
    rzp = [copy(zp_send.at[0, :, A], zp_rcv.at[0, :, A], dz(1))]
    rzm = [copy(zp_send.at[0, :, B], zm_rcv.at[0, :, B], dz(7))]

    def ring(step):
        rzp[step - 1].wait_recv()
        rzm[step - 1].wait_recv()
        if step == 1:
            zp_send[1, :, A] = (pi_own[3, :, A] + zp_rcv[0, :, A].astype(F32)).astype(BF)
            zp_send[1, :, B] = pi_own[3, :, B].astype(BF)
            zm_send[1, :, B] = (pi_own[5, :, B] + zm_rcv[0, :, B].astype(F32)).astype(BF)
            zm_send[1, :, A] = pi_own[5, :, A].astype(BF)
        else:
            zp_send[step] = (pi_own[4 - step] + zp_rcv[step - 1].astype(F32)).astype(BF)
            zm_send[step] = (pi_own[4 + step] + zm_rcv[step - 1].astype(F32)).astype(BF)
        rzp.append(copy(zp_send.at[step], zp_rcv.at[step], dz(1)))
        rzm.append(copy(zm_send.at[step], zm_rcv.at[step], dz(7)))

    ring(1)
    ring(2)

    for k in (1, 2, 3):
        sa[k].wait_recv()
    ga = a_own[...] + a_rcv[0].astype(F32) + a_rcv[1].astype(F32) + a_rcv[2].astype(F32)
    a2_send[...] = ga[1:].astype(BF)
    a2 = [copy(a2_send.at[k - 1], a2_rcv.at[3 - k], dy(k)) for k in (1, 2, 3)]
    for cp in sb.values():
        cp.wait_recv()
    gb = b_own[...] + b_rcv[0].astype(F32) + b_rcv[1].astype(F32) + b_rcv[2].astype(F32)
    b2_send[...] = gb[1:].astype(BF)
    b2 = [copy(b2_send.at[k - 1], b2_rcv.at[3 - k], dx(k)) for k in (1, 2, 3)]
    ga0 = ga[0]
    gb0 = gb[0]

    for cp in lxc:
        cp.wait_recv()
    ly[0] = (lx[0] + lx[2]) + (lx[1] + lx[3])
    lyc = [copy(ly.at[0], ly.at[4 - k], dy(k)) for k in (1, 2, 3)]

    ring(3)

    for cp in a2:
        cp.wait_recv()
    for cp in b2:
        cp.wait_recv()
    ga0 = ga0 + a2_rcv[0].astype(F32) + a2_rcv[1].astype(F32) + a2_rcv[2].astype(F32)
    gb0 = gb0 + b2_rcv[0].astype(F32) + b2_rcv[1].astype(F32) + b2_rcv[2].astype(F32)

    def back(m, ga, gb):
        ua = full[m, :, A]
        ub = full[m, :, B]
        inner = jnp.sum(ua * ga, axis=1, keepdims=True) + jnp.sum(ub * gb, axis=1, keepdims=True)
        norm = norms[m, :, 0:1]
        pgf[m, :, A] = ((ga - ua * inner) / norm).astype(BF)
        pgf[m, :, B] = ((gb - ub * inner) / norm).astype(BF)

    def share(m):
        cp = copy(pgf.at[m, :, their_cols], pg64.at[m, mine], fs_partner)
        pg64[m, mine, :] = pgf[m, :, my_cols]
        return cp

    back(1, ga0, gb0)

    def quarter(y_):
        return pl.ds(pl.multiple_of(384 * y_, 128), 384)

    pp = [
        copy(
            pgf.at[1, :, quarter(lax.rem(y + j, 4))],
            pg_plane.at[(4 - i) % 4, (4 - j) % 4], dxy(i, j),
        )
        for i, j in ORDER
    ]
    pg_plane[0, 0] = pgf[1, :, quarter(y)]
    pg_txt = share(1)

    rzp[3].wait_recv()
    rzm[3].wait_recv()
    gi = pi_own[0] + zp_rcv[3].astype(F32) + zm_rcv[3].astype(F32)
    back(0, gi[:, :H], gi[:, H:])
    pg_img = share(0)

    my_feat = pl.ds(pl.multiple_of(yh * FH, 16), FH)
    their_feat = pl.ds(pl.multiple_of((1 - yh) * FH, 16), FH)

    def feature_terms(m, w, out, into):
        out[...] = dot_nt(pg64[m], w[their_feat, :]).astype(out.dtype)
        return copy(out, into, fs_partner)

    for cp in lyc:
        cp.wait_recv()
    lc[0] = (ly[0] + ly[2]) + (ly[1] + ly[3])
    lcc = copy(lc.at[0], lc.at[1], other)
    for cp in fw:
        cp.wait_recv()
    for cp in pp:
        cp.wait_recv()
    wg[0:512, :] = dot_tn(feat_win[...].reshape(16 * R, 512), pg_plane[...].reshape(16 * R, 384))
    wg[512:528, :] = jnp.zeros((16, 384), F32)
    start = 352 * x - (256 * x + 128 * (x // 2))

    def rows16(k, core):
        first = start + 22 * k + 11 * core
        low = first // 8
        block = wg[pl.ds(pl.multiple_of(low * 8, 8), 24), :]
        return pltpu.roll(block, 24 - (first - low * 8), 0)[:16]

    def cut(k, carry):
        cw_send[k] = rows16(k, 1 - c).astype(BF)
        return carry

    lax.fori_loop(0, 16, cut, 0, unroll=4)
    cw = copy(cw_send, cw_rcv, other)

    pg_txt.wait_recv()
    fg_txt = feature_terms(1, w_txt, ft_send, ft_rcv)
    pg_img.wait_recv()
    fg_img = feature_terms(0, w_img, fi_send, fi_rcv)
    lcc.wait_recv()
    lz[0] = lc[0] + lc[1]
    lzc = [copy(lz.at[0], lz.at[8 - k], dz(k)) for k in range(1, 8)]

    cw.wait_recv()

    def add_core(k, carry):
        s2[k] = (rows16(k, c) + cw_rcv[k].astype(F32)).astype(BF)
        return carry

    lax.fori_loop(0, 16, add_core, 0, unroll=4)
    zw = []
    for k in (4, 3, 5, 2, 6, 1, 7, 0):
        zz = lax.rem(z + k, 8)
        zw.append(copy(s2.at[(1 - yl) * 8 + zz], zw_rcv.at[1, (8 - k) % 8], dyz(k)))
        if k:
            zw.append(copy(s2.at[yl * 8 + zz], zw_rcv.at[0, 8 - k], dz(k)))

    txt_out[...] = dot_nt(pg64[1], w_txt[my_feat, :])
    img_out[...] = dot_nt(pg64[0], w_img[my_feat, :])

    near = rows16(yl * 8 + z, c) + cw_rcv[yl * 8 + z].astype(F32)
    fg_txt.wait_recv()
    txt_out[...] += ft_rcv[...].astype(F32)
    for cp in lzc:
        cp.wait_recv()
    total = ((lz[0] + lz[4]) + (lz[2] + lz[6])) + ((lz[1] + lz[5]) + (lz[3] + lz[7]))
    loss_out[0] = jnp.max(total) / 8192.0
    for cp in zw:
        cp.wait_recv()
    far = zw_rcv[1, 0].astype(F32)
    for k in range(1, 8):
        near = near + zw_rcv[0, k].astype(F32)
        far = far + zw_rcv[1, k].astype(F32)
    wg_out[:, pl.ds(pl.multiple_of(384 * yl, 128), 384)] = near[:11, :]
    wg_out[:, pl.ds(pl.multiple_of(384 * (1 - yl), 128), 384)] = far[:11, :]
    fg_img.wait_recv()
    img_out[...] += fi_rcv[...]
    for cp in sent:
        cp.wait_send()


def hand_out(*refs):
    refs[4][0] = refs[0][0]
    for i in (1, 2, 3):
        refs[4 + i][...] = refs[i][...]


def body(img_feat, txt_feat, img_weight, txt_weight, logit_scale, logit_bias):
    vm = pl.BlockSpec(memory_space=pltpu.VMEM)
    sm = pl.BlockSpec(memory_space=pltpu.SMEM)
    hbm = pl.BlockSpec(memory_space=pltpu.HBM)
    V = pltpu.VMEM
    results = pl.pallas_call(
        kernel,
        out_shape=(
            jax.ShapeDtypeStruct((1,), F32),
            jax.ShapeDtypeStruct((64, FH), F32),
            jax.ShapeDtypeStruct((64, FH), F32),
            jax.ShapeDtypeStruct((11, H), F32),
        ),
        in_specs=[vm, vm, hbm, hbm, hbm, hbm],
        out_specs=(sm, vm, vm, vm),
        scratch_shapes=[
            V((64, FEAT), BF), V((64, FEAT), BF), V((FEAT, H), BF), V((FEAT, H), BF),
            V((2, 64, H), F32), V((2, R, H), F32), V((2, R, E), F32), V((2, R, 128), F32),
            V((4, 4, R, E), BF), V((2, 8, R, E), BF), V((16 * R, 16 * R), BF), V((4, 4, R, 512), BF),
            V((3, 4, R, H), BF), V((3, 4, R, H), BF), V((4, R, H), F32), V((3, R, H), BF), V((3, R, H), BF),
            V((3, 4, R, H), BF), V((3, 4, R, H), BF), V((4, R, H), F32), V((3, R, H), BF), V((3, R, H), BF),
            V((8, R, E), BF), V((8, R, E), BF), V((8, R, E), F32),
            V((4, R, E), BF), V((4, R, E), BF), V((4, R, E), BF), V((4, R, E), BF),
            V((2, R, E), BF), V((2, 64, H), BF), V((4, 4, R, 384), BF), V((64, FH), F32), V((64, FH), F32), V((64, FH), BF), V((64, FH), BF),
            V((528, 384), F32), V((16, 16, 384), BF), V((16, 16, 384), BF), V((16, 16, 384), BF), V((2, 8, 16, 384), BF),
            V((4, 8, 128), F32), V((4, 8, 128), F32), V((2, 8, 128), F32), V((8, 8, 128), F32),
            V((16 * R, 16 * R), F32),
            pltpu.SemaphoreType.DMA((N_SEM,)),
            pltpu.SemaphoreType.DMA((N_SEM,)),
            pltpu.SemaphoreType.DMA((4,)),
        ],
        compiler_params=pltpu.CompilerParams(
            collective_id=0, has_side_effects=True, vmem_limit_bytes=56 * 1024 * 1024
        ),
        name="fused",
    )(logit_scale.reshape(1, 1), logit_bias.reshape(1, 1), img_feat, txt_feat, img_weight, txt_weight)
    loss, img_grad, txt_grad, w_grad = pl.pallas_call(
        hand_out,
        out_shape=tuple(jax.ShapeDtypeStruct(r.shape, r.dtype) for r in results),
        in_specs=[sm, vm, vm, vm],
        out_specs=(sm, vm, vm, vm),
        name="hand_out",
    )(*results)
    return loss.reshape(()), img_grad, txt_grad, w_grad


def solution(mesh):
    placed = (P("dp", None), P("dp", None), P(None, "fsdp"), P(None, "fsdp"), P(), P())
    return jax.shard_map(
        body,
        mesh=mesh,
        in_specs=placed,
        out_specs=(P(), P("dp", "fsdp"), P("dp", "fsdp"), P("dp", "fsdp")),
        check_vma=False,
    )
```

```python
import jax
import jax.numpy as jnp
from jax import lax
from jax.experimental import pallas as pl
from jax.experimental.pallas import tpu as pltpu
from jax.sharding import PartitionSpec as P

EPS = 1e-06
MESH = pl.DeviceIdType.MESH
BF = jnp.bfloat16
F32 = jnp.float32
R = 32
E = 1536
H = 768
FEAT = 1408
FH = 704
N_SEM = 192
ORDER = [(2, 2), (2, 1), (2, 3), (1, 2), (3, 2), (1, 1), (1, 3), (3, 1), (3, 3), (2, 0), (0, 2), (1, 0), (3, 0), (0, 1), (0, 3)]


def dot_nt(a, b):
    return lax.dot_general(a, b, (((1,), (1,)), ((), ())), preferred_element_type=F32)


def dot_tn(a, b):
    return lax.dot_general(a, b, (((0,), (0,)), ((), ())), preferred_element_type=F32)


def kernel(
    scale_ref, bias_ref, img_f_hbm, txt_f_hbm, img_w_hbm, txt_w_hbm,
    loss_out, img_out, txt_out, wg_out,
    img_feat, txt_feat, w_img, w_txt, proj, proj_rcv, full, norms,
    txt_all, img_all, slope_s, feat_win, feat_y,
    a_send, a_rcv, a_own, a2_send, a2_rcv,
    b_send, b_rcv, b_own, b2_send, b2_rcv,
    ci_send, ci_rcv, pi_own, zp_send, zp_rcv, zm_send, zm_rcv,
    pgf, pg64, pg_plane, fi_send, fi_rcv, ft_send, ft_rcv,
    wg, cw_send, cw_rcv, s2, zw_rcv,
    lx, ly, lc, lz, logit_s,
    ssem, rsem, wsem,
):
    dp = lax.axis_index("dp")
    yh = lax.axis_index("fsdp")
    c = lax.rem(dp, 2)
    z = lax.rem(dp // 2, 8)
    yl = lax.rem(dp // 16, 2)
    x = dp // 32
    y = yh * 2 + yl

    def dev(x_, y_, z_, c_):
        return {"dp": ((x_ * 2 + lax.rem(y_, 2)) * 8 + z_) * 2 + c_, "fsdp": y_ // 2}

    def dx(k):
        return dev(lax.rem(x + k, 4), y, z, c)

    def dy(k):
        return dev(x, lax.rem(y + k, 4), z, c)

    def dz(k):
        return dev(x, y, lax.rem(z + k, 8), c)

    other = dev(x, y, z, 1 - c)
    fs_partner = dy(2)

    def dxy(i, j):
        return dev(lax.rem(x + i, 4), lax.rem(y + j, 4), z, c)

    def dyz(k):
        return dev(x, yh * 2 + (1 - yl), lax.rem(z + k, 8), c)

    counter = [0]

    def copy(src, dst, target):
        i = counter[0]
        counter[0] += 1
        cp = pltpu.make_async_remote_copy(
            src_ref=src, dst_ref=dst, send_sem=ssem.at[i], recv_sem=rsem.at[i],
            device_id=target, device_id_type=MESH,
        )
        cp.start()
        sent.append(cp)
        return cp

    sent = []

    loads = [
        pltpu.make_async_copy(img_f_hbm, img_feat, wsem.at[0]),
        pltpu.make_async_copy(img_w_hbm, w_img, wsem.at[1]),
        pltpu.make_async_copy(txt_f_hbm, txt_feat, wsem.at[2]),
        pltpu.make_async_copy(txt_w_hbm, w_txt, wsem.at[3]),
    ]
    for load in loads:
        load.start()

    barrier = pltpu.get_barrier_semaphore()
    partners = [dx(k) for k in (1, 2, 3)] + [dy(k) for k in (1, 2, 3)]
    partners += [dz(1), dz(7), other]
    for p in partners:
        pl.semaphore_signal(barrier, inc=1, device_id=p, device_id_type=MESH)

    mine = pl.ds(pl.multiple_of(yh * R, R), R)
    theirs = pl.ds(pl.multiple_of((1 - yh) * R, R), R)
    my_cols = pl.ds(pl.multiple_of(yh * H, 128), H)
    their_cols = pl.ds(pl.multiple_of((1 - yh) * H, 128), H)

    def window(x_):
        return pl.ds(pl.multiple_of(256 * x_ + 128 * (x_ // 2), 128), 512)

    loads[0].wait()
    loads[1].wait()
    proj[0] = jnp.dot(img_feat[...], w_img[...], preferred_element_type=F32)
    pl.semaphore_wait(barrier, len(partners))
    swap_img = copy(proj.at[0, theirs], proj_rcv.at[0], fs_partner)
    loads[2].wait()
    loads[3].wait()
    proj[1] = jnp.dot(txt_feat[...], w_txt[...], preferred_element_type=F32)
    swap_txt = copy(proj.at[1, theirs], proj_rcv.at[1], fs_partner)

    fw = []
    fy = [copy(txt_feat.at[mine], feat_y.at[1], dy(1)), copy(txt_feat.at[mine], feat_y.at[0], dy(3))]

    def features(own, i):
        cols = window(lax.rem(x + i, 4))
        slot = (4 - i) % 4
        sources = (txt_feat.at[mine, cols], feat_y.at[0, :, cols], txt_feat.at[theirs, cols], feat_y.at[1, :, cols])
        for j in (0, 2) if own else (1, 3):
            if i:
                fw.append(copy(sources[j], feat_win.at[slot, j], dx(i)))
            else:
                feat_win[0, j] = sources[j][...]

    for i in (2, 1, 3, 0):
        features(True, i)

    def embed(m):
        own = proj[m, mine, :]
        got = proj_rcv[m]
        total = jnp.sum(own * own, axis=1, keepdims=True) + jnp.sum(got * got, axis=1, keepdims=True)
        norm = jnp.sqrt(total + EPS)
        norms[m] = jnp.broadcast_to(norm, (R, 128))
        full[m, :, my_cols] = own / norm
        full[m, :, their_cols] = got / norm
        return full[m].astype(BF)

    A = pl.ds(0, H)
    B = pl.ds(H, H)

    zp = {}
    zm = {}
    cf = {}

    swap_img.wait_recv()
    img_all[0, 0] = embed(0)
    parts = [pl.ds(384 * q, 384) for q in range(4)]
    for q, part in enumerate(parts):
        zp[1, q] = copy(img_all.at[0, 0, :, part], img_all.at[0, 7, :, part], dz(1))
        zm[1, q] = copy(img_all.at[0, 0, :, part], img_all.at[0, 1, :, part], dz(7))
    cf[0] = copy(img_all.at[0, 0], img_all.at[1, 0], other)
    swap_txt.wait_recv()
    txt_all[0, 0] = embed(1)
    ax = {}
    ay = {}
    bx = {}
    by = {}
    for k in (1, 3, 2):
        ax[k] = copy(txt_all.at[0, 0, :, A], txt_all.at[4 - k, 0, :, A], dx(k))
        by[k] = copy(txt_all.at[0, 0, :, B], txt_all.at[0, 4 - k, :, B], dy(k))
    for k in (1, 3, 2):
        ay[0, k] = copy(txt_all.at[0, 0, :, A], txt_all.at[0, 4 - k, :, A], dy(k))
        bx[0, k] = copy(txt_all.at[0, 0, :, B], txt_all.at[4 - k, 0, :, B], dx(k))

    def second(k):
        slot = 4 - k
        ax[k].wait_recv()
        for j in (1, 3, 2):
            ay[slot, j] = copy(txt_all.at[slot, 0, :, A], txt_all.at[slot, 4 - j, :, A], dy(j))
        by[k].wait_recv()
        for j in (1, 3, 2):
            bx[slot, j] = copy(txt_all.at[0, slot, :, B], txt_all.at[4 - j, slot, :, B], dx(j))

    def along_z(step):
        for q, part in enumerate(parts):
            zp[step, q].wait_recv()
            if step < 3 or q < 2:
                zp[step + 1, q] = copy(img_all.at[0, 8 - step, :, part], img_all.at[0, 7 - step, :, part], dz(1))
            zm[step, q].wait_recv()
            if step < 3 or q >= 2:
                zm[step + 1, q] = copy(img_all.at[0, step, :, part], img_all.at[0, step + 1, :, part], dz(7))
        cf[8 - step] = copy(img_all.at[0, 8 - step], img_all.at[1, 8 - step], other)
        cf[step] = copy(img_all.at[0, step], img_all.at[1, step], other)

    along_z(1)
    second(1)
    second(3)
    along_z(2)
    second(2)
    along_z(3)
    for q in (0, 1):
        zp[4, q].wait_recv()
        zm[4, q + 2].wait_recv()
    cf[4] = copy(img_all.at[0, 4], img_all.at[1, 4], other)
    for s in range(4):
        for j in (1, 2, 3):
            ay[s, j].wait_recv()
            bx[s, j].wait_recv()

    for cp in fy:
        cp.wait_recv()
    for i in (2, 1, 3, 0):
        features(False, i)

    scale = scale_ref[...]
    bias = bias_ref[...]
    txt_rows = txt_all[...].reshape(16 * R, E)
    def strip(i, acc, diagonal):
        rows = pl.ds(pl.multiple_of(i * R, R), R)
        v = scale * logit_s[rows, :] + bias
        if diagonal:
            ri = lax.broadcasted_iota(jnp.int32, v.shape, 0)
            ci = lax.broadcasted_iota(jnp.int32, v.shape, 1)
            v = jnp.where(ri == ci, -v, v)
        t = jnp.exp(-jnp.abs(v))
        grad = scale * (jnp.where(v >= 0, 1.0, t) / (1.0 + t))
        if diagonal:
            grad = jnp.where(ri == ci, -grad, grad)
        slope_s[rows, :] = grad.astype(BF)
        m = jnp.maximum(v, 0.0)
        prod = t[0:8]
        for j in (8, 16, 24):
            prod = prod + t[j:j + 8] * (1.0 + prod)
        return acc + jnp.log1p(prod) + ((m[0:8] + m[8:16]) + (m[16:24] + m[24:32]))

    logit_s[0:8 * R, :] = dot_nt(img_all[0].reshape(8 * R, E), txt_rows)
    acc = strip(0, jnp.zeros((8, 16 * R), F32), True)
    acc = lax.fori_loop(1, 8, lambda i, a: strip(i, a, False), acc, unroll=True)
    for s in range(8):
        cf[s].wait_recv()
    logit_s[8 * R:, :] = dot_nt(img_all[1].reshape(8 * R, E), txt_rows)
    acc = lax.fori_loop(8, 16, lambda i, a: strip(i, a, False), acc, unroll=4)
    img_rows = img_all[...].reshape(16 * R, E)

    sa = {}
    sb = {}

    def text_grads(k):
        g = dot_tn(slope_s[:, k * 128:(k + 1) * 128], img_rows)
        ga = g[:, :H].reshape(4, R, H)
        gb = g[:, H:].reshape(4, R, H)
        if k:
            a_send[k - 1] = ga.astype(BF)
            sa[k] = copy(a_send.at[k - 1, 1:], a_rcv.at[3 - k, 1:], dx(k))
        else:
            a_own[...] = ga
        b_own[k] = gb[0]
        b_send[:, k] = gb[1:].astype(BF)
        for j in (1, 3, 2):
            sb[j, k] = copy(b_send.at[j - 1, k], b_rcv.at[3 - j, k], dy(j))

    text_grads(1)
    text_grads(3)
    ci_send[...] = jnp.dot(
        slope_s[8 * R:, :], txt_rows, preferred_element_type=F32
    ).astype(BF).reshape(8, R, E)
    ci_copy = copy(ci_send, ci_rcv, other)
    text_grads(2)
    text_grads(0)
    for k in (1, 3, 2):
        sa[k, 0] = copy(a_send.at[k - 1, 0], a_rcv.at[3 - k, 0], dx(k))

    pi_own[...] = jnp.dot(slope_s[:8 * R, :], txt_rows, preferred_element_type=F32).reshape(8, R, E)

    part = jnp.sum(acc)
    lx[0] = jnp.full((8, 128), part, F32)
    lxc = [copy(lx.at[0], lx.at[4 - k], dx(k)) for k in (1, 2, 3)]

    ci_copy.wait_recv()
    pi_own[...] += ci_rcv[...].astype(F32)

    rzp = {}
    rzm = {}

    def send_p(step, q, value):
        zp_send[step, :, parts[q]] = value.astype(BF)
        rzp[step, q] = copy(zp_send.at[step, :, parts[q]], zp_rcv.at[step, :, parts[q]], dz(1))

    def send_m(step, q, value):
        zm_send[step, :, parts[q]] = value.astype(BF)
        rzm[step, q] = copy(zm_send.at[step, :, parts[q]], zm_rcv.at[step, :, parts[q]], dz(7))

    for q in (0, 1):
        send_p(0, q, pi_own[4, :, parts[q]])
        send_m(0, q + 2, pi_own[4, :, parts[q + 2]])
    for q in (0, 1):
        send_p(1, q + 2, pi_own[3, :, parts[q + 2]])
        send_m(1, q, pi_own[5, :, parts[q]])

    def ring(step):
        for q in (0, 1) if step == 1 else (2, 3, 0, 1):
            r = (q + 2) % 4
            rzp[step - 1, q].wait_recv()
            send_p(step, q, pi_own[4 - step, :, parts[q]] + zp_rcv[step - 1, :, parts[q]].astype(F32))
            rzm[step - 1, r].wait_recv()
            send_m(step, r, pi_own[4 + step, :, parts[r]] + zm_rcv[step - 1, :, parts[r]].astype(F32))

    ring(1)

    def summed(own, got):
        return own + got[0].astype(F32) + got[1].astype(F32) + got[2].astype(F32)

    for k in (1, 2, 3):
        sa[k].wait_recv()
    a2_send[...] = summed(a_own[1:], [a_rcv[k, 1:] for k in range(3)]).astype(BF)
    a2 = [copy(a2_send.at[k - 1], a2_rcv.at[3 - k], dy(k)) for k in (1, 2, 3)]
    for k in (1, 2, 3):
        for j in (1, 2, 3):
            sb[j, k].wait_recv()
    b2_send[...] = summed(b_own[1:], [b_rcv[k, 1:] for k in range(3)]).astype(BF)
    b2 = [copy(b2_send.at[k - 1], b2_rcv.at[3 - k], dx(k)) for k in (1, 2, 3)]
    for k in (1, 2, 3):
        sa[k, 0].wait_recv()
        sb[k, 0].wait_recv()
    ga0 = summed(a_own[0], [a_rcv[k, 0] for k in range(3)])
    gb0 = summed(b_own[0], [b_rcv[k, 0] for k in range(3)])

    for cp in lxc:
        cp.wait_recv()
    ly[0] = (lx[0] + lx[2]) + (lx[1] + lx[3])
    lyc = [copy(ly.at[0], ly.at[4 - k], dy(k)) for k in (1, 2, 3)]

    ring(2)
    ring(3)

    for cp in a2:
        cp.wait_recv()
    for cp in b2:
        cp.wait_recv()
    ga0 = summed(ga0, a2_rcv)
    gb0 = summed(gb0, b2_rcv)

    def back(m, ga, gb):
        ua = full[m, :, A]
        ub = full[m, :, B]
        inner = jnp.sum(ua * ga, axis=1, keepdims=True) + jnp.sum(ub * gb, axis=1, keepdims=True)
        norm = norms[m, :, 0:1]
        pgf[m, :, A] = ((ga - ua * inner) / norm).astype(BF)
        pgf[m, :, B] = ((gb - ub * inner) / norm).astype(BF)

    def share(m):
        cp = copy(pgf.at[m, :, their_cols], pg64.at[m, mine], fs_partner)
        pg64[m, mine, :] = pgf[m, :, my_cols]
        return cp

    back(1, ga0, gb0)
    pg_txt = share(1)

    def quarter(y_):
        return pl.ds(pl.multiple_of(384 * y_, 128), 384)

    pp = [
        copy(
            pgf.at[1, :, quarter(lax.rem(y + j, 4))],
            pg_plane.at[(4 - i) % 4, (4 - j) % 4], dxy(i, j),
        )
        for i, j in ORDER
    ]
    pg_plane[0, 0] = pgf[1, :, quarter(y)]

    for q in range(4):
        rzp[3, q].wait_recv()
        rzm[3, q].wait_recv()
    gi = pi_own[0] + zp_rcv[3].astype(F32) + zm_rcv[3].astype(F32)
    back(0, gi[:, :H], gi[:, H:])
    pg_img = share(0)

    my_feat = pl.ds(pl.multiple_of(yh * FH, 16), FH)
    their_feat = pl.ds(pl.multiple_of((1 - yh) * FH, 16), FH)

    def feature_terms(m, w, out, into):
        out[...] = dot_nt(pg64[m], w[their_feat, :]).astype(out.dtype)
        return copy(out, into, fs_partner)

    pg_txt.wait_recv()
    fg_txt = feature_terms(1, w_txt, ft_send, ft_rcv)
    for cp in lyc:
        cp.wait_recv()
    lc[0] = (ly[0] + ly[2]) + (ly[1] + ly[3])
    lcc = copy(lc.at[0], lc.at[1], other)
    for cp in fw:
        cp.wait_recv()
    for cp in pp:
        cp.wait_recv()
    wg[0:512, :] = dot_tn(feat_win[...].reshape(16 * R, 512), pg_plane[...].reshape(16 * R, 384))
    wg[512:528, :] = jnp.zeros((16, 384), F32)
    start = 352 * x - (256 * x + 128 * (x // 2))

    def rows16(k, core):
        first = start + 22 * k + 11 * core
        low = first // 8
        block = wg[pl.ds(pl.multiple_of(low * 8, 8), 24), :]
        return pltpu.roll(block, 24 - (first - low * 8), 0)[:16]

    def cut(k, carry):
        cw_send[k] = rows16(k, 1 - c).astype(BF)
        return carry

    lax.fori_loop(0, 16, cut, 0, unroll=4)
    cw = copy(cw_send, cw_rcv, other)

    pg_img.wait_recv()
    fg_img = feature_terms(0, w_img, fi_send, fi_rcv)
    lcc.wait_recv()
    lz[0] = lc[0] + lc[1]
    lzc = [copy(lz.at[0], lz.at[8 - k], dz(k)) for k in range(1, 8)]

    cw.wait_recv()

    def add_core(k, carry):
        s2[k] = (rows16(k, c) + cw_rcv[k].astype(F32)).astype(BF)
        return carry

    lax.fori_loop(0, 16, add_core, 0, unroll=4)
    zw = []
    for k in (4, 3, 5, 2, 6, 1, 7, 0):
        zz = lax.rem(z + k, 8)
        zw.append(copy(s2.at[(1 - yl) * 8 + zz], zw_rcv.at[1, (8 - k) % 8], dyz(k)))
        if k:
            zw.append(copy(s2.at[yl * 8 + zz], zw_rcv.at[0, 8 - k], dz(k)))

    txt_out[...] = dot_nt(pg64[1], w_txt[my_feat, :])
    img_out[...] = dot_nt(pg64[0], w_img[my_feat, :])

    near = rows16(yl * 8 + z, c) + cw_rcv[yl * 8 + z].astype(F32)
    fg_txt.wait_recv()
    txt_out[...] += ft_rcv[...].astype(F32)
    for cp in lzc:
        cp.wait_recv()
    total = ((lz[0] + lz[4]) + (lz[2] + lz[6])) + ((lz[1] + lz[5]) + (lz[3] + lz[7]))
    loss_out[0] = jnp.max(total) / 8192.0
    for cp in zw:
        cp.wait_recv()
    far = zw_rcv[1, 0].astype(F32)
    for k in range(1, 8):
        near = near + zw_rcv[0, k].astype(F32)
        far = far + zw_rcv[1, k].astype(F32)
    wg_out[:, pl.ds(pl.multiple_of(384 * yl, 128), 384)] = near[:11, :]
    wg_out[:, pl.ds(pl.multiple_of(384 * (1 - yl), 128), 384)] = far[:11, :]
    fg_img.wait_recv()
    img_out[...] += fi_rcv[...]
    for cp in sent:
        cp.wait_send()


def hand_out(*refs):
    refs[4][0] = refs[0][0]
    for i in (1, 2, 3):
        refs[4 + i][...] = refs[i][...]


def body(img_feat, txt_feat, img_weight, txt_weight, logit_scale, logit_bias):
    vm = pl.BlockSpec(memory_space=pltpu.VMEM)
    sm = pl.BlockSpec(memory_space=pltpu.SMEM)
    hbm = pl.BlockSpec(memory_space=pltpu.HBM)
    V = pltpu.VMEM
    results = pl.pallas_call(
        kernel,
        out_shape=(
            jax.ShapeDtypeStruct((1,), F32),
            jax.ShapeDtypeStruct((64, FH), F32),
            jax.ShapeDtypeStruct((64, FH), F32),
            jax.ShapeDtypeStruct((11, H), F32),
        ),
        in_specs=[vm, vm, hbm, hbm, hbm, hbm],
        out_specs=(sm, vm, vm, vm),
        scratch_shapes=[
            V((64, FEAT), BF), V((64, FEAT), BF), V((FEAT, H), BF), V((FEAT, H), BF),
            V((2, 64, H), F32), V((2, R, H), F32), V((2, R, E), F32), V((2, R, 128), F32),
            V((4, 4, R, E), BF), V((2, 8, R, E), BF), V((16 * R, 16 * R), BF), V((4, 4, R, 512), BF), V((2, R, FEAT), BF),
            V((3, 4, R, H), BF), V((3, 4, R, H), BF), V((4, R, H), F32), V((3, R, H), BF), V((3, R, H), BF),
            V((3, 4, R, H), BF), V((3, 4, R, H), BF), V((4, R, H), F32), V((3, R, H), BF), V((3, R, H), BF),
            V((8, R, E), BF), V((8, R, E), BF), V((8, R, E), F32),
            V((4, R, E), BF), V((4, R, E), BF), V((4, R, E), BF), V((4, R, E), BF),
            V((2, R, E), BF), V((2, 64, H), BF), V((4, 4, R, 384), BF), V((64, FH), F32), V((64, FH), F32), V((64, FH), BF), V((64, FH), BF),
            V((528, 384), F32), V((16, 16, 384), BF), V((16, 16, 384), BF), V((16, 16, 384), BF), V((2, 8, 16, 384), BF),
            V((4, 8, 128), F32), V((4, 8, 128), F32), V((2, 8, 128), F32), V((8, 8, 128), F32),
            V((16 * R, 16 * R), F32),
            pltpu.SemaphoreType.DMA((N_SEM,)),
            pltpu.SemaphoreType.DMA((N_SEM,)),
            pltpu.SemaphoreType.DMA((4,)),
        ],
        compiler_params=pltpu.CompilerParams(
            collective_id=0, has_side_effects=True, vmem_limit_bytes=56 * 1024 * 1024
        ),
        name="fused",
    )(logit_scale.reshape(1, 1), logit_bias.reshape(1, 1), img_feat, txt_feat, img_weight, txt_weight)
    loss, img_grad, txt_grad, w_grad = pl.pallas_call(
        hand_out,
        out_shape=tuple(jax.ShapeDtypeStruct(r.shape, r.dtype) for r in results),
        in_specs=[sm, vm, vm, vm],
        out_specs=(sm, vm, vm, vm),
        name="hand_out",
    )(*results)
    return loss.reshape(()), img_grad, txt_grad, w_grad


def solution(mesh):
    placed = (P("dp", None), P("dp", None), P(None, "fsdp"), P(None, "fsdp"), P(), P())
    return jax.shard_map(
        body,
        mesh=mesh,
        in_specs=placed,
        out_specs=(P(), P("dp", "fsdp"), P("dp", "fsdp"), P("dp", "fsdp")),
        check_vma=False,
    )
```

```python
import jax
import jax.numpy as jnp
from jax import lax
from jax.experimental import pallas as pl
from jax.experimental.pallas import tpu as pltpu
from jax.sharding import PartitionSpec as P

EPS = 1e-06
MESH = pl.DeviceIdType.MESH
BF = jnp.bfloat16
F32 = jnp.float32
R = 32
E = 1536
H = 768
FEAT = 1408
FH = 704
N_SEM = 240
ORDER = [(2, 2), (2, 1), (2, 3), (1, 2), (3, 2), (1, 1), (1, 3), (3, 1), (3, 3), (2, 0), (0, 2), (1, 0), (3, 0), (0, 1), (0, 3)]


def dot_nt(a, b):
    return lax.dot_general(a, b, (((1,), (1,)), ((), ())), preferred_element_type=F32)


def dot_tn(a, b):
    return lax.dot_general(a, b, (((0,), (0,)), ((), ())), preferred_element_type=F32)


def kernel(
    scale_ref, bias_ref, img_f_hbm, txt_f_hbm, img_w_hbm, txt_w_hbm,
    loss_out, img_out, txt_out, wg_out,
    img_feat, txt_feat, w_img, w_txt, proj, proj_rcv, full, norms,
    txt_all, img_all, slope_s, feat_win, feat_y,
    a_mid, b_mid, a_send, a_rcv, a_own, a2_send, a2_rcv,
    b_send, b_rcv, b_own, b2_send, b2_rcv,
    ci_send, ci_rcv, pi_own, zp_send, zp_rcv, zm_send, zm_rcv,
    pgf, pg64, pg_plane, fi_send, fi_rcv, ft_send, ft_rcv,
    wg, cw_send, cw_rcv, s2, zw_rcv,
    lx, ly, lc, lz, logit_s,
    ssem, rsem, wsem,
):
    dp = lax.axis_index("dp")
    yh = lax.axis_index("fsdp")
    c = lax.rem(dp, 2)
    z = lax.rem(dp // 2, 8)
    yl = lax.rem(dp // 16, 2)
    x = dp // 32
    y = yh * 2 + yl

    def dev(x_, y_, z_, c_):
        return {"dp": ((x_ * 2 + lax.rem(y_, 2)) * 8 + z_) * 2 + c_, "fsdp": y_ // 2}

    def dx(k):
        return dev(lax.rem(x + k, 4), y, z, c)

    def dy(k):
        return dev(x, lax.rem(y + k, 4), z, c)

    def dz(k):
        return dev(x, y, lax.rem(z + k, 8), c)

    other = dev(x, y, z, 1 - c)
    fs_partner = dy(2)

    def dxy(i, j):
        return dev(lax.rem(x + i, 4), lax.rem(y + j, 4), z, c)

    def dyz(k):
        return dev(x, yh * 2 + (1 - yl), lax.rem(z + k, 8), c)

    counter = [0]

    def copy(src, dst, target):
        i = counter[0]
        counter[0] += 1
        cp = pltpu.make_async_remote_copy(
            src_ref=src, dst_ref=dst, send_sem=ssem.at[i], recv_sem=rsem.at[i],
            device_id=target, device_id_type=MESH,
        )
        cp.start()
        sent.append(cp)
        return cp

    sent = []

    loads = [
        pltpu.make_async_copy(img_f_hbm, img_feat, wsem.at[0]),
        pltpu.make_async_copy(img_w_hbm, w_img, wsem.at[1]),
        pltpu.make_async_copy(txt_f_hbm, txt_feat, wsem.at[2]),
        pltpu.make_async_copy(txt_w_hbm, w_txt, wsem.at[3]),
    ]
    for load in loads:
        load.start()

    barrier = pltpu.get_barrier_semaphore()
    partners = [dx(k) for k in (1, 2, 3)] + [dy(k) for k in (1, 2, 3)]
    partners += [dz(1), dz(7), other]
    for p in partners:
        pl.semaphore_signal(barrier, inc=1, device_id=p, device_id_type=MESH)

    mine = pl.ds(pl.multiple_of(yh * R, R), R)
    theirs = pl.ds(pl.multiple_of((1 - yh) * R, R), R)
    my_cols = pl.ds(pl.multiple_of(yh * H, 128), H)
    their_cols = pl.ds(pl.multiple_of((1 - yh) * H, 128), H)

    def window(x_):
        return pl.ds(pl.multiple_of(256 * x_ + 128 * (x_ // 2), 128), 512)

    loads[0].wait()
    loads[1].wait()
    proj[0] = jnp.dot(img_feat[...], w_img[...], preferred_element_type=F32)
    pl.semaphore_wait(barrier, len(partners))
    swap_img = copy(proj.at[0, theirs], proj_rcv.at[0], fs_partner)
    loads[2].wait()
    loads[3].wait()
    proj[1] = jnp.dot(txt_feat[...], w_txt[...], preferred_element_type=F32)
    swap_txt = copy(proj.at[1, theirs], proj_rcv.at[1], fs_partner)

    fw = []
    fy = [copy(txt_feat.at[mine], feat_y.at[1], dy(1)), copy(txt_feat.at[mine], feat_y.at[0], dy(3))]

    def features(own, i):
        cols = window(lax.rem(x + i, 4))
        slot = (4 - i) % 4
        sources = (txt_feat.at[mine, cols], feat_y.at[0, :, cols], txt_feat.at[theirs, cols], feat_y.at[1, :, cols])
        for j in (0, 2) if own else (1, 3):
            if i:
                fw.append(copy(sources[j], feat_win.at[slot, j], dx(i)))
            else:
                feat_win[0, j] = sources[j][...]

    for i in (2, 1, 3, 0):
        features(True, i)

    def embed(m):
        own = proj[m, mine, :]
        got = proj_rcv[m]
        total = jnp.sum(own * own, axis=1, keepdims=True) + jnp.sum(got * got, axis=1, keepdims=True)
        norm = jnp.sqrt(total + EPS)
        norms[m] = jnp.broadcast_to(norm, (R, 128))
        full[m, :, my_cols] = own / norm
        full[m, :, their_cols] = got / norm
        return full[m].astype(BF)

    A = pl.ds(0, H)
    B = pl.ds(H, H)

    zp = {}
    zm = {}
    cf = {}

    swap_img.wait_recv()
    img_all[0, 0] = embed(0)
    parts = [pl.ds(384 * q, 384) for q in range(4)]
    for q, part in enumerate(parts):
        zp[1, q] = copy(img_all.at[0, 0, :, part], img_all.at[0, 7, :, part], dz(1))
        zm[1, q] = copy(img_all.at[0, 0, :, part], img_all.at[0, 1, :, part], dz(7))
    cf[0] = copy(img_all.at[0, 0], img_all.at[1, 0], other)
    swap_txt.wait_recv()
    txt_all[0, 0] = embed(1)
    ax = {}
    ay = {}
    bx = {}
    by = {}
    for k in (1, 3, 2):
        ax[k] = copy(txt_all.at[0, 0, :, A], txt_all.at[4 - k, 0, :, A], dx(k))
        by[k] = copy(txt_all.at[0, 0, :, B], txt_all.at[0, 4 - k, :, B], dy(k))
    for k in (1, 3, 2):
        ay[0, k] = copy(txt_all.at[0, 0, :, A], txt_all.at[0, 4 - k, :, A], dy(k))
        bx[0, k] = copy(txt_all.at[0, 0, :, B], txt_all.at[4 - k, 0, :, B], dx(k))

    def second(k):
        slot = 4 - k
        ax[k].wait_recv()
        for j in (1, 3, 2):
            ay[slot, j] = copy(txt_all.at[slot, 0, :, A], txt_all.at[slot, 4 - j, :, A], dy(j))
        by[k].wait_recv()
        for j in (1, 3, 2):
            bx[slot, j] = copy(txt_all.at[0, slot, :, B], txt_all.at[4 - j, slot, :, B], dx(j))

    def along_z(step):
        for q, part in enumerate(parts):
            zp[step, q].wait_recv()
            if step < 3 or q < 2:
                zp[step + 1, q] = copy(img_all.at[0, 8 - step, :, part], img_all.at[0, 7 - step, :, part], dz(1))
            zm[step, q].wait_recv()
            if step < 3 or q >= 2:
                zm[step + 1, q] = copy(img_all.at[0, step, :, part], img_all.at[0, step + 1, :, part], dz(7))
        cf[8 - step] = copy(img_all.at[0, 8 - step], img_all.at[1, 8 - step], other)
        cf[step] = copy(img_all.at[0, step], img_all.at[1, step], other)

    along_z(1)
    second(1)
    second(3)
    along_z(2)
    second(2)
    along_z(3)
    for q in (0, 1):
        zp[4, q].wait_recv()
        zm[4, q + 2].wait_recv()
    cf[4] = copy(img_all.at[0, 4], img_all.at[1, 4], other)
    for s in range(4):
        for j in (1, 2, 3):
            ay[s, j].wait_recv()
            bx[s, j].wait_recv()

    for cp in fy:
        cp.wait_recv()
    for i in (2, 1, 3, 0):
        features(False, i)

    scale = scale_ref[...]
    bias = bias_ref[...]
    txt_rows = txt_all[...].reshape(16 * R, E)
    def strip(i, acc, diagonal):
        rows = pl.ds(pl.multiple_of(i * R, R), R)
        v = scale * logit_s[rows, :] + bias
        if diagonal:
            ri = lax.broadcasted_iota(jnp.int32, v.shape, 0)
            ci = lax.broadcasted_iota(jnp.int32, v.shape, 1)
            v = jnp.where(ri == ci, -v, v)
        t = jnp.exp(-jnp.abs(v))
        grad = scale * (jnp.where(v >= 0, 1.0, t) / (1.0 + t))
        if diagonal:
            grad = jnp.where(ri == ci, -grad, grad)
        slope_s[rows, :] = grad.astype(BF)
        m = jnp.maximum(v, 0.0)
        prod = t[0:8]
        for j in (8, 16, 24):
            prod = prod + t[j:j + 8] * (1.0 + prod)
        return acc + jnp.log1p(prod) + ((m[0:8] + m[8:16]) + (m[16:24] + m[24:32]))

    logit_s[0:8 * R, :] = dot_nt(img_all[0].reshape(8 * R, E), txt_rows)
    acc = strip(0, jnp.zeros((8, 16 * R), F32), True)
    acc = lax.fori_loop(1, 8, lambda i, a: strip(i, a, False), acc, unroll=True)
    for s in range(8):
        cf[s].wait_recv()
    logit_s[8 * R:, :] = dot_nt(img_all[1].reshape(8 * R, E), txt_rows)
    acc = lax.fori_loop(8, 16, lambda i, a: strip(i, a, False), acc, unroll=4)
    img_rows = img_all[...].reshape(16 * R, E)

    left = pl.ds(0, 384)
    right = pl.ds(384, 384)
    sa = {}
    sb = {}

    def text_grads(k):
        g = dot_tn(slope_s[:, k * 128:(k + 1) * 128], img_rows)
        ga = g[:, :H].reshape(4, R, H)
        gb = g[:, H:].reshape(4, R, H)
        if k == 2:
            a_send[1] = ga.astype(BF)
            sa["far", 1] = copy(a_send.at[1, :, :, left], a_rcv.at[1, :, :, left], dx(1))
            sa["far", 3] = copy(a_send.at[1, :, :, right], a_rcv.at[1, :, :, right], dx(3))
        elif k == 1:
            a_mid[0] = ga[:, :, :384]
            a_send[0, :, :, right] = ga[:, :, 384:].astype(BF)
            sa["near", 1] = copy(a_send.at[0, :, :, right], a_rcv.at[0, :, :, right], dx(1))
        elif k == 3:
            a_mid[1] = ga[:, :, 384:]
            a_send[2, :, :, left] = ga[:, :, :384].astype(BF)
            sa["near", 3] = copy(a_send.at[2, :, :, left], a_rcv.at[2, :, :, left], dx(3))
        else:
            a_own[...] = ga
        b_own[k] = gb[0]
        b_send[1, k] = gb[2].astype(BF)
        sb["far", 1, k] = copy(b_send.at[1, k, :, left], b_rcv.at[1, k, :, left], dy(1))
        sb["far", 3, k] = copy(b_send.at[1, k, :, right], b_rcv.at[1, k, :, right], dy(3))
        b_mid[0, k] = gb[1, :, :384]
        b_mid[1, k] = gb[3, :, 384:]
        b_send[0, k, :, right] = gb[1, :, 384:].astype(BF)
        b_send[2, k, :, left] = gb[3, :, :384].astype(BF)
        sb["near", 1, k] = copy(b_send.at[0, k, :, right], b_rcv.at[0, k, :, right], dy(1))
        sb["near", 3, k] = copy(b_send.at[2, k, :, left], b_rcv.at[2, k, :, left], dy(3))

    def relay_a():
        for way, mid, cols in ((1, 0, left), (3, 1, right)):
            sa["far", way].wait_recv()
            a_send[way - 1, :, :, cols] = (a_mid[mid] + a_rcv[1, :, :, cols].astype(F32)).astype(BF)
            sa["sum", way] = copy(a_send.at[way - 1, 1:, :, cols], a_rcv.at[way - 1, 1:, :, cols], dx(way))
        for way, cols in ((1, left), (3, right)):
            sa["own", way] = copy(a_send.at[way - 1, 0, :, cols], a_rcv.at[way - 1, 0, :, cols], dx(way))

    def relay_b(k):
        for way, mid, cols in ((1, 0, left), (3, 1, right)):
            sb["far", way, k].wait_recv()
            b_send[way - 1, k, :, cols] = (b_mid[mid, k] + b_rcv[1, k, :, cols].astype(F32)).astype(BF)
            sb["sum", way, k] = copy(b_send.at[way - 1, k, :, cols], b_rcv.at[way - 1, k, :, cols], dy(way))

    text_grads(2)
    text_grads(1)
    ci_send[...] = jnp.dot(
        slope_s[8 * R:, :], txt_rows, preferred_element_type=F32
    ).astype(BF).reshape(8, R, E)
    ci_copy = copy(ci_send, ci_rcv, other)
    text_grads(3)
    text_grads(0)
    relay_b(2)
    pi_own[...] = jnp.dot(slope_s[:8 * R, :], txt_rows, preferred_element_type=F32).reshape(8, R, E)
    relay_b(1)

    part = jnp.sum(acc)
    lx[0] = jnp.full((8, 128), part, F32)
    lxc = [copy(lx.at[0], lx.at[4 - k], dx(k)) for k in (1, 2, 3)]

    ci_copy.wait_recv()
    pi_own[...] += ci_rcv[...].astype(F32)

    rzp = {}
    rzm = {}

    def send_p(step, q, value):
        zp_send[step, :, parts[q]] = value.astype(BF)
        rzp[step, q] = copy(zp_send.at[step, :, parts[q]], zp_rcv.at[step, :, parts[q]], dz(1))

    def send_m(step, q, value):
        zm_send[step, :, parts[q]] = value.astype(BF)
        rzm[step, q] = copy(zm_send.at[step, :, parts[q]], zm_rcv.at[step, :, parts[q]], dz(7))

    for q in (0, 1):
        send_p(0, q, pi_own[4, :, parts[q]])
        send_m(0, q + 2, pi_own[4, :, parts[q + 2]])
    for q in (0, 1):
        send_p(1, q + 2, pi_own[3, :, parts[q + 2]])
        send_m(1, q, pi_own[5, :, parts[q]])

    def ring(step):
        for q in (0, 1) if step == 1 else (2, 3, 0, 1):
            r = (q + 2) % 4
            rzp[step - 1, q].wait_recv()
            send_p(step, q, pi_own[4 - step, :, parts[q]] + zp_rcv[step - 1, :, parts[q]].astype(F32))
            rzm[step - 1, r].wait_recv()
            send_m(step, r, pi_own[4 + step, :, parts[r]] + zm_rcv[step - 1, :, parts[r]].astype(F32))

    relay_a()
    relay_b(3)
    relay_b(0)
    ring(1)

    def summed(own, *got):
        for part in got:
            own = own + part.astype(F32)
        return own

    for way in (1, 3):
        sa["near", way].wait_recv()
        sa["sum", way].wait_recv()
    a2_send[...] = summed(a_own[1:], a_rcv[0, 1:], a_rcv[2, 1:]).astype(BF)
    a2 = [copy(a2_send.at[k - 1], a2_rcv.at[3 - k], dy(k)) for k in (1, 2, 3)]
    for way in (1, 3):
        for k in (1, 2, 3):
            sb["near", way, k].wait_recv()
            sb["sum", way, k].wait_recv()
    b2_send[...] = summed(b_own[1:], b_rcv[0, 1:], b_rcv[2, 1:]).astype(BF)
    b2 = [copy(b2_send.at[k - 1], b2_rcv.at[3 - k], dx(k)) for k in (1, 2, 3)]
    for way in (1, 3):
        sa["own", way].wait_recv()
        sb["near", way, 0].wait_recv()
        sb["sum", way, 0].wait_recv()
    ga0 = summed(a_own[0], a_rcv[0, 0], a_rcv[2, 0])
    gb0 = summed(b_own[0], b_rcv[0, 0], b_rcv[2, 0])

    for cp in lxc:
        cp.wait_recv()
    ly[0] = (lx[0] + lx[2]) + (lx[1] + lx[3])
    lyc = [copy(ly.at[0], ly.at[4 - k], dy(k)) for k in (1, 2, 3)]

    ring(2)
    ring(3)

    for cp in a2:
        cp.wait_recv()
    for cp in b2:
        cp.wait_recv()
    ga0 = summed(ga0, a2_rcv[0], a2_rcv[1], a2_rcv[2])
    gb0 = summed(gb0, b2_rcv[0], b2_rcv[1], b2_rcv[2])

    def back(m, ga, gb):
        ua = full[m, :, A]
        ub = full[m, :, B]
        inner = jnp.sum(ua * ga, axis=1, keepdims=True) + jnp.sum(ub * gb, axis=1, keepdims=True)
        norm = norms[m, :, 0:1]
        pgf[m, :, A] = ((ga - ua * inner) / norm).astype(BF)
        pgf[m, :, B] = ((gb - ub * inner) / norm).astype(BF)

    def share(m):
        cp = copy(pgf.at[m, :, their_cols], pg64.at[m, mine], fs_partner)
        pg64[m, mine, :] = pgf[m, :, my_cols]
        return cp

    back(1, ga0, gb0)
    pg_txt = share(1)

    def quarter(y_):
        return pl.ds(pl.multiple_of(384 * y_, 128), 384)

    pp = [
        copy(
            pgf.at[1, :, quarter(lax.rem(y + j, 4))],
            pg_plane.at[(4 - i) % 4, (4 - j) % 4], dxy(i, j),
        )
        for i, j in ORDER
    ]
    pg_plane[0, 0] = pgf[1, :, quarter(y)]

    for q in range(4):
        rzp[3, q].wait_recv()
        rzm[3, q].wait_recv()
    gi = pi_own[0] + zp_rcv[3].astype(F32) + zm_rcv[3].astype(F32)
    back(0, gi[:, :H], gi[:, H:])
    pg_img = share(0)

    my_feat = pl.ds(pl.multiple_of(yh * FH, 16), FH)
    their_feat = pl.ds(pl.multiple_of((1 - yh) * FH, 16), FH)

    def feature_terms(m, w, out, into):
        out[...] = dot_nt(pg64[m], w[their_feat, :]).astype(out.dtype)
        return copy(out, into, fs_partner)

    pg_txt.wait_recv()
    fg_txt = feature_terms(1, w_txt, ft_send, ft_rcv)
    for cp in lyc:
        cp.wait_recv()
    lc[0] = (ly[0] + ly[2]) + (ly[1] + ly[3])
    lcc = copy(lc.at[0], lc.at[1], other)
    for cp in fw:
        cp.wait_recv()
    for cp in pp:
        cp.wait_recv()
    wg[0:512, :] = dot_tn(feat_win[...].reshape(16 * R, 512), pg_plane[...].reshape(16 * R, 384))
    wg[512:528, :] = jnp.zeros((16, 384), F32)
    start = 352 * x - (256 * x + 128 * (x // 2))

    def rows16(k, core):
        first = start + 22 * k + 11 * core
        low = first // 8
        block = wg[pl.ds(pl.multiple_of(low * 8, 8), 24), :]
        return pltpu.roll(block, 24 - (first - low * 8), 0)[:16]

    def cut(k, carry):
        cw_send[k] = rows16(k, 1 - c).astype(BF)
        return carry

    lax.fori_loop(0, 16, cut, 0, unroll=4)
    cw = copy(cw_send, cw_rcv, other)

    lcc.wait_recv()
    lz[0] = lc[0] + lc[1]
    lzc = [copy(lz.at[0], lz.at[8 - k], dz(k)) for k in range(1, 8)]

    cw.wait_recv()

    def add_core(k, carry):
        s2[k] = (rows16(k, c) + cw_rcv[k].astype(F32)).astype(BF)
        return carry

    lax.fori_loop(0, 16, add_core, 0, unroll=4)
    zw = []
    for k in (4, 3, 5, 2, 6, 1, 7, 0):
        zz = lax.rem(z + k, 8)
        zw.append(copy(s2.at[(1 - yl) * 8 + zz], zw_rcv.at[1, (8 - k) % 8], dyz(k)))
        if k:
            zw.append(copy(s2.at[yl * 8 + zz], zw_rcv.at[0, 8 - k], dz(k)))

    pg_img.wait_recv()
    fg_img = feature_terms(0, w_img, fi_send, fi_rcv)
    txt_out[...] = dot_nt(pg64[1], w_txt[my_feat, :])
    img_out[...] = dot_nt(pg64[0], w_img[my_feat, :])

    near = rows16(yl * 8 + z, c) + cw_rcv[yl * 8 + z].astype(F32)
    fg_txt.wait_recv()
    txt_out[...] += ft_rcv[...].astype(F32)
    for cp in lzc:
        cp.wait_recv()
    total = ((lz[0] + lz[4]) + (lz[2] + lz[6])) + ((lz[1] + lz[5]) + (lz[3] + lz[7]))
    loss_out[0] = jnp.max(total) / 8192.0
    for cp in zw:
        cp.wait_recv()
    far = zw_rcv[1, 0].astype(F32)
    for k in range(1, 8):
        near = near + zw_rcv[0, k].astype(F32)
        far = far + zw_rcv[1, k].astype(F32)
    wg_out[:, pl.ds(pl.multiple_of(384 * yl, 128), 384)] = near[:11, :]
    wg_out[:, pl.ds(pl.multiple_of(384 * (1 - yl), 128), 384)] = far[:11, :]
    fg_img.wait_recv()
    img_out[...] += fi_rcv[...].astype(F32)
    assert counter[0] <= N_SEM
    for cp in sent:
        cp.wait_send()


def hand_out(*refs):
    refs[4][0] = refs[0][0]
    for i in (1, 2, 3):
        refs[4 + i][...] = refs[i][...]


def body(img_feat, txt_feat, img_weight, txt_weight, logit_scale, logit_bias):
    vm = pl.BlockSpec(memory_space=pltpu.VMEM)
    sm = pl.BlockSpec(memory_space=pltpu.SMEM)
    hbm = pl.BlockSpec(memory_space=pltpu.HBM)
    V = pltpu.VMEM
    results = pl.pallas_call(
        kernel,
        out_shape=(
            jax.ShapeDtypeStruct((1,), F32),
            jax.ShapeDtypeStruct((64, FH), F32),
            jax.ShapeDtypeStruct((64, FH), F32),
            jax.ShapeDtypeStruct((11, H), F32),
        ),
        in_specs=[vm, vm, hbm, hbm, hbm, hbm],
        out_specs=(sm, vm, vm, vm),
        scratch_shapes=[
            V((64, FEAT), BF), V((64, FEAT), BF), V((FEAT, H), BF), V((FEAT, H), BF),
            V((2, 64, H), F32), V((2, R, H), F32), V((2, R, E), F32), V((2, R, 128), F32),
            V((4, 4, R, E), BF), V((2, 8, R, E), BF), V((16 * R, 16 * R), BF), V((4, 4, R, 512), BF), V((2, R, FEAT), BF),
            V((2, 4, R, 384), F32), V((2, 4, R, 384), F32),
            V((3, 4, R, H), BF), V((3, 4, R, H), BF), V((4, R, H), F32), V((3, R, H), BF), V((3, R, H), BF),
            V((3, 4, R, H), BF), V((3, 4, R, H), BF), V((4, R, H), F32), V((3, R, H), BF), V((3, R, H), BF),
            V((8, R, E), BF), V((8, R, E), BF), V((8, R, E), F32),
            V((4, R, E), BF), V((4, R, E), BF), V((4, R, E), BF), V((4, R, E), BF),
            V((2, R, E), BF), V((2, 64, H), BF), V((4, 4, R, 384), BF), V((64, FH), BF), V((64, FH), BF), V((64, FH), BF), V((64, FH), BF),
            V((528, 384), F32), V((16, 16, 384), BF), V((16, 16, 384), BF), V((16, 16, 384), BF), V((2, 8, 16, 384), BF),
            V((4, 8, 128), F32), V((4, 8, 128), F32), V((2, 8, 128), F32), V((8, 8, 128), F32),
            V((16 * R, 16 * R), F32),
            pltpu.SemaphoreType.DMA((N_SEM,)),
            pltpu.SemaphoreType.DMA((N_SEM,)),
            pltpu.SemaphoreType.DMA((4,)),
        ],
        compiler_params=pltpu.CompilerParams(
            collective_id=0, has_side_effects=True, vmem_limit_bytes=56 * 1024 * 1024
        ),
        name="fused",
    )(logit_scale.reshape(1, 1), logit_bias.reshape(1, 1), img_feat, txt_feat, img_weight, txt_weight)
    loss, img_grad, txt_grad, w_grad = pl.pallas_call(
        hand_out,
        out_shape=tuple(jax.ShapeDtypeStruct(r.shape, r.dtype) for r in results),
        in_specs=[sm, vm, vm, vm],
        out_specs=(sm, vm, vm, vm),
        name="hand_out",
    )(*results)
    return loss.reshape(()), img_grad, txt_grad, w_grad


def solution(mesh):
    placed = (P("dp", None), P("dp", None), P(None, "fsdp"), P(None, "fsdp"), P(), P())
    return jax.shard_map(
        body,
        mesh=mesh,
        in_specs=placed,
        out_specs=(P(), P("dp", "fsdp"), P("dp", "fsdp"), P("dp", "fsdp")),
        check_vma=False,
    )
```

```python
import jax
import jax.numpy as jnp
from jax import lax
from jax.experimental import pallas as pl
from jax.experimental.pallas import tpu as pltpu
from jax.sharding import PartitionSpec as P

EPS = 1e-06
MESH = pl.DeviceIdType.MESH
BF = jnp.bfloat16
F32 = jnp.float32
R = 32
E = 1536
H = 768
FEAT = 1408
FH = 704
N_SEM = 240
ORDER = [(2, 2), (2, 1), (2, 3), (1, 2), (3, 2), (1, 1), (1, 3), (3, 1), (3, 3), (2, 0), (0, 2), (1, 0), (3, 0), (0, 1), (0, 3)]


def dot_nt(a, b):
    return lax.dot_general(a, b, (((1,), (1,)), ((), ())), preferred_element_type=F32)


def dot_tn(a, b):
    return lax.dot_general(a, b, (((0,), (0,)), ((), ())), preferred_element_type=F32)


def kernel(
    scale_ref, bias_ref, img_f_hbm, txt_f_hbm, img_w_hbm, txt_w_hbm,
    loss_out, img_out, txt_out, wg_out,
    img_feat, txt_feat, w_img, w_txt, proj, proj_rcv, full, norms,
    txt_all, img_all, slope_s, feat_win, feat_y,
    a_mid, b_mid, a_send, a_rcv, a_own, a2_send, a2_rcv,
    b_send, b_rcv, b_own, b2_send, b2_rcv,
    ci_send, ci_rcv, pi_own, zp_send, zp_rcv, zm_send, zm_rcv,
    pgf, pg64, pg_plane, fi_send, fi_rcv, ft_send, ft_rcv,
    wg, cw_send, cw_rcv, s2, zw_rcv,
    lx, ly, lc, lz, logit_s,
    ssem, rsem, wsem,
):
    dp = lax.axis_index("dp")
    yh = lax.axis_index("fsdp")
    c = lax.rem(dp, 2)
    z = lax.rem(dp // 2, 8)
    yl = lax.rem(dp // 16, 2)
    x = dp // 32
    y = yh * 2 + yl

    def dev(x_, y_, z_, c_):
        return {"dp": ((x_ * 2 + lax.rem(y_, 2)) * 8 + z_) * 2 + c_, "fsdp": y_ // 2}

    def dx(k):
        return dev(lax.rem(x + k, 4), y, z, c)

    def dy(k):
        return dev(x, lax.rem(y + k, 4), z, c)

    def dz(k):
        return dev(x, y, lax.rem(z + k, 8), c)

    other = dev(x, y, z, 1 - c)
    fs_partner = dy(2)

    def dxy(i, j):
        return dev(lax.rem(x + i, 4), lax.rem(y + j, 4), z, c)

    def dyz(k):
        return dev(x, yh * 2 + (1 - yl), lax.rem(z + k, 8), c)

    counter = [0]

    def copy(src, dst, target):
        i = counter[0]
        counter[0] += 1
        cp = pltpu.make_async_remote_copy(
            src_ref=src, dst_ref=dst, send_sem=ssem.at[i], recv_sem=rsem.at[i],
            device_id=target, device_id_type=MESH,
        )
        cp.start()
        sent.append(cp)
        return cp

    sent = []

    def flush(upto):
        for cp in sent[:upto]:
            cp.wait_send()
        del sent[:upto]

    loads = [
        pltpu.make_async_copy(img_f_hbm, img_feat, wsem.at[0]),
        pltpu.make_async_copy(img_w_hbm, w_img, wsem.at[1]),
        pltpu.make_async_copy(txt_f_hbm, txt_feat, wsem.at[2]),
        pltpu.make_async_copy(txt_w_hbm, w_txt, wsem.at[3]),
    ]
    loads[1].start()
    loads[0].start()

    barrier = pltpu.get_barrier_semaphore()
    partners = [dx(k) for k in (1, 2, 3)] + [dy(k) for k in (1, 2, 3)]
    partners += [dz(1), dz(7), other]
    for p in partners:
        pl.semaphore_signal(barrier, inc=1, device_id=p, device_id_type=MESH)

    mine = pl.ds(pl.multiple_of(yh * R, R), R)
    theirs = pl.ds(pl.multiple_of((1 - yh) * R, R), R)
    my_cols = pl.ds(pl.multiple_of(yh * H, 128), H)
    their_cols = pl.ds(pl.multiple_of((1 - yh) * H, 128), H)

    def window(x_):
        return pl.ds(pl.multiple_of(256 * x_ + 128 * (x_ // 2), 128), 512)

    loads[0].wait()
    loads[3].start()
    loads[2].start()
    loads[1].wait()
    proj[0] = jnp.dot(img_feat[...], w_img[...], preferred_element_type=F32)
    pl.semaphore_wait(barrier, len(partners))
    swap_img = copy(proj.at[0, theirs], proj_rcv.at[0], fs_partner)
    loads[2].wait()
    loads[3].wait()
    proj[1] = jnp.dot(txt_feat[...], w_txt[...], preferred_element_type=F32)
    swap_txt = copy(proj.at[1, theirs], proj_rcv.at[1], fs_partner)

    fw = []
    fy = [copy(txt_feat.at[mine], feat_y.at[1], dy(1)), copy(txt_feat.at[mine], feat_y.at[0], dy(3))]

    def features(own, i):
        cols = window(lax.rem(x + i, 4))
        slot = (4 - i) % 4
        sources = (txt_feat.at[mine, cols], feat_y.at[0, :, cols], txt_feat.at[theirs, cols], feat_y.at[1, :, cols])
        for j in (0, 2) if own else (1, 3):
            if i:
                fw.append(copy(sources[j], feat_win.at[slot, j], dx(i)))
            else:
                feat_win[0, j] = sources[j][...]

    for i in (2, 1, 3, 0):
        features(True, i)

    def embed(m):
        own = proj[m, mine, :]
        got = proj_rcv[m]
        total = jnp.sum(own * own, axis=1, keepdims=True) + jnp.sum(got * got, axis=1, keepdims=True)
        norm = jnp.sqrt(total + EPS)
        norms[m] = jnp.broadcast_to(norm, (R, 128))
        full[m, :, my_cols] = own / norm
        full[m, :, their_cols] = got / norm
        return full[m].astype(BF)

    A = pl.ds(0, H)
    B = pl.ds(H, H)

    zp = {}
    zm = {}
    cf = {}

    swap_img.wait_recv()
    img_all[0, 0] = embed(0)
    parts = [pl.ds(384 * q, 384) for q in range(4)]
    for q, part in enumerate(parts):
        zp[1, q] = copy(img_all.at[0, 0, :, part], img_all.at[0, 7, :, part], dz(1))
        zm[1, q] = copy(img_all.at[0, 0, :, part], img_all.at[0, 1, :, part], dz(7))
    cf[0] = copy(img_all.at[0, 0], img_all.at[1, 0], other)
    swap_txt.wait_recv()
    txt_all[0, 0] = embed(1)
    ax = {}
    ay = {}
    bx = {}
    by = {}
    for k in (1, 3, 2):
        ax[k] = copy(txt_all.at[0, 0, :, A], txt_all.at[4 - k, 0, :, A], dx(k))
        by[k] = copy(txt_all.at[0, 0, :, B], txt_all.at[0, 4 - k, :, B], dy(k))
    for k in (1, 3, 2):
        ay[0, k] = copy(txt_all.at[0, 0, :, A], txt_all.at[0, 4 - k, :, A], dy(k))
        bx[0, k] = copy(txt_all.at[0, 0, :, B], txt_all.at[4 - k, 0, :, B], dx(k))

    def second(k):
        slot = 4 - k
        ax[k].wait_recv()
        for j in (1, 3, 2):
            ay[slot, j] = copy(txt_all.at[slot, 0, :, A], txt_all.at[slot, 4 - j, :, A], dy(j))
        by[k].wait_recv()
        for j in (1, 3, 2):
            bx[slot, j] = copy(txt_all.at[0, slot, :, B], txt_all.at[4 - j, slot, :, B], dx(j))

    def along_z(step):
        for q, part in enumerate(parts):
            zp[step, q].wait_recv()
            if step < 3 or q < 2:
                zp[step + 1, q] = copy(img_all.at[0, 8 - step, :, part], img_all.at[0, 7 - step, :, part], dz(1))
            zm[step, q].wait_recv()
            if step < 3 or q >= 2:
                zm[step + 1, q] = copy(img_all.at[0, step, :, part], img_all.at[0, step + 1, :, part], dz(7))
            if q % 2:
                cols = (A, B)[q // 2]
                for slot in (8 - step, step):
                    cf[slot, q] = copy(img_all.at[0, slot, :, cols], img_all.at[1, slot, :, cols], other)

    along_z(1)
    second(1)
    second(3)
    along_z(2)
    second(2)
    along_z(3)
    for way, cols, q in ((zp, A, 0), (zm, B, 2)):
        way[4, q].wait_recv()
        way[4, q + 1].wait_recv()
        cf[4, q] = copy(img_all.at[0, 4, :, cols], img_all.at[1, 4, :, cols], other)
    for s in range(4):
        for j in (1, 2, 3):
            ay[s, j].wait_recv()
            bx[s, j].wait_recv()

    for cp in fy:
        cp.wait_recv()
    for i in (2, 1, 3, 0):
        features(False, i)

    scale = scale_ref[...]
    bias = bias_ref[...]
    txt_rows = txt_all[...].reshape(16 * R, E)
    def strip(i, acc, diagonal):
        rows = pl.ds(pl.multiple_of(i * R, R), R)
        v = scale * logit_s[rows, :] + bias
        if diagonal:
            ri = lax.broadcasted_iota(jnp.int32, v.shape, 0)
            ci = lax.broadcasted_iota(jnp.int32, v.shape, 1)
            v = jnp.where(ri == ci, -v, v)
        t = jnp.exp(-jnp.abs(v))
        grad = scale * (jnp.where(v >= 0, 1.0, t) / (1.0 + t))
        if diagonal:
            grad = jnp.where(ri == ci, -grad, grad)
        slope_s[rows, :] = grad.astype(BF)
        m = jnp.maximum(v, 0.0)
        prod = t[0:8]
        for j in (8, 16, 24):
            prod = prod + t[j:j + 8] * (1.0 + prod)
        return acc + jnp.log1p(prod) + ((m[0:8] + m[8:16]) + (m[16:24] + m[24:32]))

    logit_s[0:8 * R, :] = dot_nt(img_all[0].reshape(8 * R, E), txt_rows)
    acc = strip(0, jnp.zeros((8, 16 * R), F32), True)
    acc = lax.fori_loop(1, 8, lambda i, a: strip(i, a, False), acc, unroll=True)
    for cp in cf.values():
        cp.wait_recv()
    logit_s[8 * R:, :] = dot_nt(img_all[1].reshape(8 * R, E), txt_rows)
    acc = lax.fori_loop(8, 16, lambda i, a: strip(i, a, False), acc, unroll=4)
    img_rows = img_all[...].reshape(16 * R, E)

    left = pl.ds(0, 384)
    right = pl.ds(384, 384)
    sa = {}
    sb = {}

    def text_grads(k):
        g = dot_tn(slope_s[:, k * 128:(k + 1) * 128], img_rows)
        ga = g[:, :H].reshape(4, R, H)
        gb = g[:, H:].reshape(4, R, H)
        if k == 2:
            a_send[1] = ga.astype(BF)
            sa["far", 1] = copy(a_send.at[1, :, :, left], a_rcv.at[1, :, :, left], dx(1))
            sa["far", 3] = copy(a_send.at[1, :, :, right], a_rcv.at[1, :, :, right], dx(3))
        elif k == 1:
            a_mid[0] = ga[:, :, :384]
            a_send[0, :, :, right] = ga[:, :, 384:].astype(BF)
            sa["near", 1] = copy(a_send.at[0, :, :, right], a_rcv.at[0, :, :, right], dx(1))
        elif k == 3:
            a_mid[1] = ga[:, :, 384:]
            a_send[2, :, :, left] = ga[:, :, :384].astype(BF)
            sa["near", 3] = copy(a_send.at[2, :, :, left], a_rcv.at[2, :, :, left], dx(3))
        else:
            a_own[...] = ga
        b_own[k] = gb[0]
        b_send[1, k] = gb[2].astype(BF)
        sb["far", 1, k] = copy(b_send.at[1, k, :, left], b_rcv.at[1, k, :, left], dy(1))
        sb["far", 3, k] = copy(b_send.at[1, k, :, right], b_rcv.at[1, k, :, right], dy(3))
        b_mid[0, k] = gb[1, :, :384]
        b_mid[1, k] = gb[3, :, 384:]
        b_send[0, k, :, right] = gb[1, :, 384:].astype(BF)
        b_send[2, k, :, left] = gb[3, :, :384].astype(BF)
        sb["near", 1, k] = copy(b_send.at[0, k, :, right], b_rcv.at[0, k, :, right], dy(1))
        sb["near", 3, k] = copy(b_send.at[2, k, :, left], b_rcv.at[2, k, :, left], dy(3))

    def relay_a():
        for way, mid, cols in ((1, 0, left), (3, 1, right)):
            sa["far", way].wait_recv()
            a_send[way - 1, :, :, cols] = (a_mid[mid] + a_rcv[1, :, :, cols].astype(F32)).astype(BF)
            sa["sum", way] = copy(a_send.at[way - 1, 1:, :, cols], a_rcv.at[way - 1, 1:, :, cols], dx(way))
        for way, cols in ((1, left), (3, right)):
            sa["own", way] = copy(a_send.at[way - 1, 0, :, cols], a_rcv.at[way - 1, 0, :, cols], dx(way))

    def relay_b(k):
        for way, mid, cols in ((1, 0, left), (3, 1, right)):
            sb["far", way, k].wait_recv()
            b_send[way - 1, k, :, cols] = (b_mid[mid, k] + b_rcv[1, k, :, cols].astype(F32)).astype(BF)
            sb["sum", way, k] = copy(b_send.at[way - 1, k, :, cols], b_rcv.at[way - 1, k, :, cols], dy(way))

    text_grads(2)
    text_grads(1)
    ci_send[...] = jnp.dot(
        slope_s[8 * R:, :], txt_rows, preferred_element_type=F32
    ).astype(BF).reshape(8, R, E)
    ci_copy = copy(ci_send, ci_rcv, other)
    text_grads(3)
    text_grads(0)
    relay_b(2)
    pi_own[...] = jnp.dot(slope_s[:8 * R, :], txt_rows, preferred_element_type=F32).reshape(8, R, E)
    relay_b(1)

    part = jnp.sum(acc)
    lx[0] = jnp.full((8, 128), part, F32)
    lxc = [copy(lx.at[0], lx.at[4 - k], dx(k)) for k in (1, 2, 3)]

    ci_copy.wait_recv()
    pi_own[...] += ci_rcv[...].astype(F32)

    rzp = {}
    rzm = {}

    def send_p(step, q, value):
        zp_send[step, :, parts[q]] = value.astype(BF)
        rzp[step, q] = copy(zp_send.at[step, :, parts[q]], zp_rcv.at[step, :, parts[q]], dz(1))

    def send_m(step, q, value):
        zm_send[step, :, parts[q]] = value.astype(BF)
        rzm[step, q] = copy(zm_send.at[step, :, parts[q]], zm_rcv.at[step, :, parts[q]], dz(7))

    for q in (0, 1):
        send_p(0, q, pi_own[4, :, parts[q]])
        send_m(0, q + 2, pi_own[4, :, parts[q + 2]])
    for q in (0, 1):
        send_p(1, q + 2, pi_own[3, :, parts[q + 2]])
        send_m(1, q, pi_own[5, :, parts[q]])

    def ring(step):
        for q in (0, 1) if step == 1 else (2, 3, 0, 1):
            r = (q + 2) % 4
            rzp[step - 1, q].wait_recv()
            send_p(step, q, pi_own[4 - step, :, parts[q]] + zp_rcv[step - 1, :, parts[q]].astype(F32))
            rzm[step - 1, r].wait_recv()
            send_m(step, r, pi_own[4 + step, :, parts[r]] + zm_rcv[step - 1, :, parts[r]].astype(F32))

    relay_a()
    relay_b(3)
    relay_b(0)
    ring(1)

    def summed(own, *got):
        for part in got:
            own = own + part.astype(F32)
        return own

    for way in (1, 3):
        sa["near", way].wait_recv()
        sa["sum", way].wait_recv()
    a2_send[...] = summed(a_own[1:], a_rcv[0, 1:], a_rcv[2, 1:]).astype(BF)
    a2 = [copy(a2_send.at[k - 1], a2_rcv.at[3 - k], dy(k)) for k in (1, 2, 3)]
    for way in (1, 3):
        for k in (1, 2, 3):
            sb["near", way, k].wait_recv()
            sb["sum", way, k].wait_recv()
    b2_send[...] = summed(b_own[1:], b_rcv[0, 1:], b_rcv[2, 1:]).astype(BF)
    b2 = [copy(b2_send.at[k - 1], b2_rcv.at[3 - k], dx(k)) for k in (1, 2, 3)]
    for way in (1, 3):
        sa["own", way].wait_recv()
        sb["near", way, 0].wait_recv()
        sb["sum", way, 0].wait_recv()
    ga0 = summed(a_own[0], a_rcv[0, 0], a_rcv[2, 0])
    gb0 = summed(b_own[0], b_rcv[0, 0], b_rcv[2, 0])

    for cp in lxc:
        cp.wait_recv()
    ly[0] = (lx[0] + lx[2]) + (lx[1] + lx[3])
    lyc = [copy(ly.at[0], ly.at[4 - k], dy(k)) for k in (1, 2, 3)]

    ring(2)
    ring(3)

    for cp in a2:
        cp.wait_recv()
    for cp in b2:
        cp.wait_recv()
    ga0 = summed(ga0, a2_rcv[0], a2_rcv[1], a2_rcv[2])
    gb0 = summed(gb0, b2_rcv[0], b2_rcv[1], b2_rcv[2])

    def back(m, ga, gb):
        ua = full[m, :, A]
        ub = full[m, :, B]
        inner = jnp.sum(ua * ga, axis=1, keepdims=True) + jnp.sum(ub * gb, axis=1, keepdims=True)
        norm = norms[m, :, 0:1]
        pgf[m, :, A] = ((ga - ua * inner) / norm).astype(BF)
        pgf[m, :, B] = ((gb - ub * inner) / norm).astype(BF)

    def share(m):
        cp = copy(pgf.at[m, :, their_cols], pg64.at[m, mine], fs_partner)
        pg64[m, mine, :] = pgf[m, :, my_cols]
        return cp

    before = len(sent)
    back(1, ga0, gb0)
    pg_txt = share(1)

    def quarter(y_):
        return pl.ds(pl.multiple_of(384 * y_, 128), 384)

    pp = [
        copy(
            pgf.at[1, :, quarter(lax.rem(y + j, 4))],
            pg_plane.at[(4 - i) % 4, (4 - j) % 4], dxy(i, j),
        )
        for i, j in ORDER
    ]
    pg_plane[0, 0] = pgf[1, :, quarter(y)]

    for q in range(4):
        rzp[3, q].wait_recv()
        rzm[3, q].wait_recv()
    gi = pi_own[0] + zp_rcv[3].astype(F32) + zm_rcv[3].astype(F32)
    back(0, gi[:, :H], gi[:, H:])
    pg_img = share(0)

    my_feat = pl.ds(pl.multiple_of(yh * FH, 16), FH)
    their_feat = pl.ds(pl.multiple_of((1 - yh) * FH, 16), FH)

    def feature_terms(m, w, out, into):
        out[...] = dot_nt(pg64[m], w[their_feat, :]).astype(out.dtype)
        return copy(out, into, fs_partner)

    pg_txt.wait_recv()
    fg_txt = feature_terms(1, w_txt, ft_send, ft_rcv)
    for cp in lyc:
        cp.wait_recv()
    lc[0] = (ly[0] + ly[2]) + (ly[1] + ly[3])
    lcc = copy(lc.at[0], lc.at[1], other)
    for cp in fw:
        cp.wait_recv()
    flush(before)
    for cp in pp:
        cp.wait_recv()
    wg[0:512, :] = dot_tn(feat_win[...].reshape(16 * R, 512), pg_plane[...].reshape(16 * R, 384))
    wg[512:528, :] = jnp.zeros((16, 384), F32)
    start = 352 * x - (256 * x + 128 * (x // 2))

    def rows16(k, core):
        first = start + 22 * k + 11 * core
        low = first // 8
        block = wg[pl.ds(pl.multiple_of(low * 8, 8), 24), :]
        return pltpu.roll(block, 24 - (first - low * 8), 0)[:16]

    def cut(k, carry):
        cw_send[k] = rows16(k, 1 - c).astype(BF)
        return carry

    lax.fori_loop(0, 16, cut, 0, unroll=4)
    cw = copy(cw_send, cw_rcv, other)

    lcc.wait_recv()
    lz[0] = lc[0] + lc[1]
    lzc = [copy(lz.at[0], lz.at[8 - k], dz(k)) for k in range(1, 8)]

    cw.wait_recv()

    def add_core(k, carry):
        s2[k] = (rows16(k, c) + cw_rcv[k].astype(F32)).astype(BF)
        return carry

    lax.fori_loop(0, 16, add_core, 0, unroll=4)
    before = len(sent)
    zw = []
    for k in (4, 3, 5, 2, 6, 1, 7, 0):
        zz = lax.rem(z + k, 8)
        zw.append(copy(s2.at[(1 - yl) * 8 + zz], zw_rcv.at[1, (8 - k) % 8], dyz(k)))
        if k:
            zw.append(copy(s2.at[yl * 8 + zz], zw_rcv.at[0, 8 - k], dz(k)))

    pg_img.wait_recv()
    fg_img = feature_terms(0, w_img, fi_send, fi_rcv)
    txt_out[...] = dot_nt(pg64[1], w_txt[my_feat, :])
    img_out[...] = dot_nt(pg64[0], w_img[my_feat, :])

    near = rows16(yl * 8 + z, c) + cw_rcv[yl * 8 + z].astype(F32)
    fg_txt.wait_recv()
    txt_out[...] += ft_rcv[...].astype(F32)
    for cp in lzc:
        cp.wait_recv()
    total = ((lz[0] + lz[4]) + (lz[2] + lz[6])) + ((lz[1] + lz[5]) + (lz[3] + lz[7]))
    loss_out[0] = jnp.max(total) / 8192.0
    flush(before)
    for cp in zw:
        cp.wait_recv()
    far = zw_rcv[1, 0].astype(F32)
    for k in range(1, 8):
        near = near + zw_rcv[0, k].astype(F32)
        far = far + zw_rcv[1, k].astype(F32)
    wg_out[:, pl.ds(pl.multiple_of(384 * yl, 128), 384)] = near[:11, :]
    wg_out[:, pl.ds(pl.multiple_of(384 * (1 - yl), 128), 384)] = far[:11, :]
    fg_img.wait_recv()
    img_out[...] += fi_rcv[...].astype(F32)
    assert counter[0] <= N_SEM
    for cp in sent:
        cp.wait_send()


def hand_out(*refs):
    refs[4][0] = refs[0][0]
    for i in (1, 2, 3):
        refs[4 + i][...] = refs[i][...]


def body(img_feat, txt_feat, img_weight, txt_weight, logit_scale, logit_bias):
    vm = pl.BlockSpec(memory_space=pltpu.VMEM)
    sm = pl.BlockSpec(memory_space=pltpu.SMEM)
    hbm = pl.BlockSpec(memory_space=pltpu.HBM)
    V = pltpu.VMEM
    results = pl.pallas_call(
        kernel,
        out_shape=(
            jax.ShapeDtypeStruct((1,), F32),
            jax.ShapeDtypeStruct((64, FH), F32),
            jax.ShapeDtypeStruct((64, FH), F32),
            jax.ShapeDtypeStruct((11, H), F32),
        ),
        in_specs=[vm, vm, hbm, hbm, hbm, hbm],
        out_specs=(sm, vm, vm, vm),
        scratch_shapes=[
            V((64, FEAT), BF), V((64, FEAT), BF), V((FEAT, H), BF), V((FEAT, H), BF),
            V((2, 64, H), F32), V((2, R, H), F32), V((2, R, E), F32), V((2, R, 128), F32),
            V((4, 4, R, E), BF), V((2, 8, R, E), BF), V((16 * R, 16 * R), BF), V((4, 4, R, 512), BF), V((2, R, FEAT), BF),
            V((2, 4, R, 384), F32), V((2, 4, R, 384), F32),
            V((3, 4, R, H), BF), V((3, 4, R, H), BF), V((4, R, H), F32), V((3, R, H), BF), V((3, R, H), BF),
            V((3, 4, R, H), BF), V((3, 4, R, H), BF), V((4, R, H), F32), V((3, R, H), BF), V((3, R, H), BF),
            V((8, R, E), BF), V((8, R, E), BF), V((8, R, E), F32),
            V((4, R, E), BF), V((4, R, E), BF), V((4, R, E), BF), V((4, R, E), BF),
            V((2, R, E), BF), V((2, 64, H), BF), V((4, 4, R, 384), BF), V((64, FH), BF), V((64, FH), BF), V((64, FH), BF), V((64, FH), BF),
            V((528, 384), F32), V((16, 16, 384), BF), V((16, 16, 384), BF), V((16, 16, 384), BF), V((2, 8, 16, 384), BF),
            V((4, 8, 128), F32), V((4, 8, 128), F32), V((2, 8, 128), F32), V((8, 8, 128), F32),
            V((16 * R, 16 * R), F32),
            pltpu.SemaphoreType.DMA((N_SEM,)),
            pltpu.SemaphoreType.DMA((N_SEM,)),
            pltpu.SemaphoreType.DMA((4,)),
        ],
        compiler_params=pltpu.CompilerParams(
            collective_id=0, has_side_effects=True, vmem_limit_bytes=56 * 1024 * 1024
        ),
        name="fused",
    )(logit_scale.reshape(1, 1), logit_bias.reshape(1, 1), img_feat, txt_feat, img_weight, txt_weight)
    loss, img_grad, txt_grad, w_grad = pl.pallas_call(
        hand_out,
        out_shape=tuple(jax.ShapeDtypeStruct(r.shape, r.dtype) for r in results),
        in_specs=[sm, vm, vm, vm],
        out_specs=(sm, vm, vm, vm),
        name="hand_out",
    )(*results)
    return loss.reshape(()), img_grad, txt_grad, w_grad


def solution(mesh):
    placed = (P("dp", None), P("dp", None), P(None, "fsdp"), P(None, "fsdp"), P(), P())
    return jax.shard_map(
        body,
        mesh=mesh,
        in_specs=placed,
        out_specs=(P(), P("dp", "fsdp"), P("dp", "fsdp"), P("dp", "fsdp")),
        check_vma=False,
    )
```

```python
import jax
import jax.numpy as jnp
from jax import lax
from jax.experimental import pallas as pl
from jax.experimental.pallas import tpu as pltpu
from jax.sharding import PartitionSpec as P

EPS = 1e-06
MESH = pl.DeviceIdType.MESH
BF = jnp.bfloat16
F32 = jnp.float32
R = 32
E = 1536
H = 768
FEAT = 1408
FH = 704
N_SEM = 240
ORDER = [(2, 2), (2, 1), (2, 3), (1, 2), (3, 2), (1, 1), (1, 3), (3, 1), (3, 3), (2, 0), (0, 2), (1, 0), (3, 0), (0, 1), (0, 3)]


def dot_nt(a, b):
    return lax.dot_general(a, b, (((1,), (1,)), ((), ())), preferred_element_type=F32)


def dot_tn(a, b):
    return lax.dot_general(a, b, (((0,), (0,)), ((), ())), preferred_element_type=F32)


def kernel(
    scale_ref, bias_ref, img_f_hbm, txt_f_hbm, img_w_hbm, txt_w_hbm,
    loss_out, img_out, txt_out, wg_out,
    img_feat, txt_feat, w_img, w_txt, proj, proj_rcv, full, norms,
    txt_all, img_all, slope_s, feat_win, feat_y,
    a_mid, b_mid, a_send, a_rcv, a_own, a2_send, a2_rcv,
    b_send, b_rcv, b_own, b2_send, b2_rcv,
    ci_send, ci_rcv, pi_own, zp_send, zp_rcv, zm_send, zm_rcv,
    pgf, pg64, pg_plane, fi_send, fi_rcv, ft_send, ft_rcv,
    wg, cw_send, cw_rcv, s2, zw_rcv,
    lx, ly, lc, lz, logit_s,
    ssem, rsem, wsem,
):
    dp = lax.axis_index("dp")
    yh = lax.axis_index("fsdp")
    c = lax.rem(dp, 2)
    z = lax.rem(dp // 2, 8)
    yl = lax.rem(dp // 16, 2)
    x = dp // 32
    y = yh * 2 + yl

    def dev(x_, y_, z_, c_):
        return {"dp": ((x_ * 2 + lax.rem(y_, 2)) * 8 + z_) * 2 + c_, "fsdp": y_ // 2}

    def dx(k):
        return dev(lax.rem(x + k, 4), y, z, c)

    def dy(k):
        return dev(x, lax.rem(y + k, 4), z, c)

    def dz(k):
        return dev(x, y, lax.rem(z + k, 8), c)

    other = dev(x, y, z, 1 - c)
    fs_partner = dy(2)

    def dxy(i, j):
        return dev(lax.rem(x + i, 4), lax.rem(y + j, 4), z, c)

    def dyz(k):
        return dev(x, yh * 2 + (1 - yl), lax.rem(z + k, 8), c)

    counter = [0]

    def copy(src, dst, target):
        i = counter[0]
        counter[0] += 1
        cp = pltpu.make_async_remote_copy(
            src_ref=src, dst_ref=dst, send_sem=ssem.at[i], recv_sem=rsem.at[i],
            device_id=target, device_id_type=MESH,
        )
        cp.start()
        sent.append(cp)
        return cp

    sent = []

    def flush(upto):
        for cp in sent[:upto]:
            cp.wait_send()
        del sent[:upto]

    loads = [
        pltpu.make_async_copy(img_f_hbm, img_feat, wsem.at[0]),
        pltpu.make_async_copy(img_w_hbm, w_img, wsem.at[1]),
        pltpu.make_async_copy(txt_f_hbm, txt_feat, wsem.at[2]),
        pltpu.make_async_copy(txt_w_hbm, w_txt, wsem.at[3]),
    ]
    loads[1].start()
    loads[0].start()

    barrier = pltpu.get_barrier_semaphore()
    partners = [dx(k) for k in (1, 2, 3)] + [dy(k) for k in (1, 2, 3)]
    partners += [dz(1), dz(7), other]
    for p in partners:
        pl.semaphore_signal(barrier, inc=1, device_id=p, device_id_type=MESH)

    mine = pl.ds(pl.multiple_of(yh * R, R), R)
    theirs = pl.ds(pl.multiple_of((1 - yh) * R, R), R)
    my_cols = pl.ds(pl.multiple_of(yh * H, 128), H)
    their_cols = pl.ds(pl.multiple_of((1 - yh) * H, 128), H)

    def window(x_):
        return pl.ds(pl.multiple_of(256 * x_ + 128 * (x_ // 2), 128), 512)

    loads[0].wait()
    loads[3].start()
    loads[2].start()
    loads[1].wait()
    swap_img = []
    for cols in (pl.ds(0, 384), pl.ds(384, 384)):
        proj[0, :, cols] = jnp.dot(img_feat[...], w_img[:, cols], preferred_element_type=F32)
        if not swap_img:
            pl.semaphore_wait(barrier, len(partners))
        swap_img.append(copy(proj.at[0, theirs, cols], proj_rcv.at[0, :, cols], fs_partner))
    loads[2].wait()
    loads[3].wait()
    proj[1] = jnp.dot(txt_feat[...], w_txt[...], preferred_element_type=F32)
    swap_txt = copy(proj.at[1, theirs], proj_rcv.at[1], fs_partner)

    fw = []
    fy = [copy(txt_feat.at[mine], feat_y.at[1], dy(1)), copy(txt_feat.at[mine], feat_y.at[0], dy(3))]

    def features(own, i):
        cols = window(lax.rem(x + i, 4))
        slot = (4 - i) % 4
        sources = (txt_feat.at[mine, cols], feat_y.at[0, :, cols], txt_feat.at[theirs, cols], feat_y.at[1, :, cols])
        for j in (0, 2) if own else (1, 3):
            if i:
                fw.append(copy(sources[j], feat_win.at[slot, j], dx(i)))
            else:
                feat_win[0, j] = sources[j][...]

    for i in (2, 1, 3, 0):
        features(True, i)

    def embed(m):
        own = proj[m, mine, :]
        got = proj_rcv[m]
        total = jnp.sum(own * own, axis=1, keepdims=True) + jnp.sum(got * got, axis=1, keepdims=True)
        norm = jnp.sqrt(total + EPS)
        norms[m] = jnp.broadcast_to(norm, (R, 128))
        full[m, :, my_cols] = own / norm
        full[m, :, their_cols] = got / norm
        return full[m].astype(BF)

    A = pl.ds(0, H)
    B = pl.ds(H, H)

    zp = {}
    zm = {}
    cf = {}

    for cp in swap_img:
        cp.wait_recv()
    img_all[0, 0] = embed(0)
    parts = [pl.ds(384 * q, 384) for q in range(4)]
    for q, part in enumerate(parts):
        zp[1, q] = copy(img_all.at[0, 0, :, part], img_all.at[0, 7, :, part], dz(1))
        zm[1, q] = copy(img_all.at[0, 0, :, part], img_all.at[0, 1, :, part], dz(7))
    cf[0] = copy(img_all.at[0, 0], img_all.at[1, 0], other)
    swap_txt.wait_recv()
    txt_all[0, 0] = embed(1)
    ax = {}
    ay = {}
    bx = {}
    by = {}
    for k in (1, 3, 2):
        ax[k] = copy(txt_all.at[0, 0, :, A], txt_all.at[4 - k, 0, :, A], dx(k))
        by[k] = copy(txt_all.at[0, 0, :, B], txt_all.at[0, 4 - k, :, B], dy(k))
    for k in (1, 3, 2):
        ay[0, k] = copy(txt_all.at[0, 0, :, A], txt_all.at[0, 4 - k, :, A], dy(k))
        bx[0, k] = copy(txt_all.at[0, 0, :, B], txt_all.at[4 - k, 0, :, B], dx(k))

    def second(k):
        slot = 4 - k
        ax[k].wait_recv()
        for j in (1, 3, 2):
            ay[slot, j] = copy(txt_all.at[slot, 0, :, A], txt_all.at[slot, 4 - j, :, A], dy(j))
        by[k].wait_recv()
        for j in (1, 3, 2):
            bx[slot, j] = copy(txt_all.at[0, slot, :, B], txt_all.at[4 - j, slot, :, B], dx(j))

    def along_z(step):
        for q, part in enumerate(parts):
            zp[step, q].wait_recv()
            if step < 3 or q < 2:
                zp[step + 1, q] = copy(img_all.at[0, 8 - step, :, part], img_all.at[0, 7 - step, :, part], dz(1))
            zm[step, q].wait_recv()
            if step < 3 or q >= 2:
                zm[step + 1, q] = copy(img_all.at[0, step, :, part], img_all.at[0, step + 1, :, part], dz(7))
            if q % 2:
                cols = (A, B)[q // 2]
                for slot in (8 - step, step):
                    cf[slot, q] = copy(img_all.at[0, slot, :, cols], img_all.at[1, slot, :, cols], other)

    along_z(1)
    second(1)
    second(3)
    along_z(2)
    second(2)
    along_z(3)
    for way, cols, q in ((zp, A, 0), (zm, B, 2)):
        way[4, q].wait_recv()
        way[4, q + 1].wait_recv()
        cf[4, q] = copy(img_all.at[0, 4, :, cols], img_all.at[1, 4, :, cols], other)
    for s in range(4):
        for j in (1, 2, 3):
            ay[s, j].wait_recv()
            bx[s, j].wait_recv()

    for cp in fy:
        cp.wait_recv()
    for i in (2, 1, 3, 0):
        features(False, i)

    scale = scale_ref[...]
    bias = bias_ref[...]
    txt_rows = txt_all[...].reshape(16 * R, E)
    def strip(i, acc, diagonal):
        rows = pl.ds(pl.multiple_of(i * R, R), R)
        v = scale * logit_s[rows, :] + bias
        if diagonal:
            ri = lax.broadcasted_iota(jnp.int32, v.shape, 0)
            ci = lax.broadcasted_iota(jnp.int32, v.shape, 1)
            v = jnp.where(ri == ci, -v, v)
        t = jnp.exp(-jnp.abs(v))
        grad = scale * (jnp.where(v >= 0, 1.0, t) / (1.0 + t))
        if diagonal:
            grad = jnp.where(ri == ci, -grad, grad)
        slope_s[rows, :] = grad.astype(BF)
        m = jnp.maximum(v, 0.0)
        prod = t[0:8]
        for j in (8, 16, 24):
            prod = prod + t[j:j + 8] * (1.0 + prod)
        return acc + jnp.log1p(prod) + ((m[0:8] + m[8:16]) + (m[16:24] + m[24:32]))

    logit_s[0:8 * R, :] = dot_nt(img_all[0].reshape(8 * R, E), txt_rows)
    acc = strip(0, jnp.zeros((8, 16 * R), F32), True)
    acc = lax.fori_loop(1, 8, lambda i, a: strip(i, a, False), acc, unroll=True)
    for cp in cf.values():
        cp.wait_recv()
    logit_s[8 * R:, :] = dot_nt(img_all[1].reshape(8 * R, E), txt_rows)
    acc = lax.fori_loop(8, 16, lambda i, a: strip(i, a, False), acc, unroll=4)
    img_rows = img_all[...].reshape(16 * R, E)

    left = pl.ds(0, 384)
    right = pl.ds(384, 384)
    sa = {}
    sb = {}

    def text_grads(k):
        g = dot_tn(slope_s[:, k * 128:(k + 1) * 128], img_rows)
        ga = g[:, :H].reshape(4, R, H)
        gb = g[:, H:].reshape(4, R, H)
        if k == 2:
            a_send[1] = ga.astype(BF)
            sa["far", 1] = copy(a_send.at[1, :, :, left], a_rcv.at[1, :, :, left], dx(1))
            sa["far", 3] = copy(a_send.at[1, :, :, right], a_rcv.at[1, :, :, right], dx(3))
        elif k == 1:
            a_mid[0] = ga[:, :, :384]
            a_send[0, :, :, right] = ga[:, :, 384:].astype(BF)
            sa["near", 1] = copy(a_send.at[0, :, :, right], a_rcv.at[0, :, :, right], dx(1))
        elif k == 3:
            a_mid[1] = ga[:, :, 384:]
            a_send[2, :, :, left] = ga[:, :, :384].astype(BF)
            sa["near", 3] = copy(a_send.at[2, :, :, left], a_rcv.at[2, :, :, left], dx(3))
        else:
            a_own[...] = ga
        b_own[k] = gb[0]
        b_send[1, k] = gb[2].astype(BF)
        sb["far", 1, k] = copy(b_send.at[1, k, :, left], b_rcv.at[1, k, :, left], dy(1))
        sb["far", 3, k] = copy(b_send.at[1, k, :, right], b_rcv.at[1, k, :, right], dy(3))
        b_mid[0, k] = gb[1, :, :384]
        b_mid[1, k] = gb[3, :, 384:]
        b_send[0, k, :, right] = gb[1, :, 384:].astype(BF)
        b_send[2, k, :, left] = gb[3, :, :384].astype(BF)
        sb["near", 1, k] = copy(b_send.at[0, k, :, right], b_rcv.at[0, k, :, right], dy(1))
        sb["near", 3, k] = copy(b_send.at[2, k, :, left], b_rcv.at[2, k, :, left], dy(3))

    def relay_a():
        for way, mid, cols in ((1, 0, left), (3, 1, right)):
            sa["far", way].wait_recv()
            a_send[way - 1, :, :, cols] = (a_mid[mid] + a_rcv[1, :, :, cols].astype(F32)).astype(BF)
            sa["sum", way] = copy(a_send.at[way - 1, 1:, :, cols], a_rcv.at[way - 1, 1:, :, cols], dx(way))
        for way, cols in ((1, left), (3, right)):
            sa["own", way] = copy(a_send.at[way - 1, 0, :, cols], a_rcv.at[way - 1, 0, :, cols], dx(way))

    def relay_b(k):
        for way, mid, cols in ((1, 0, left), (3, 1, right)):
            sb["far", way, k].wait_recv()
            b_send[way - 1, k, :, cols] = (b_mid[mid, k] + b_rcv[1, k, :, cols].astype(F32)).astype(BF)
            sb["sum", way, k] = copy(b_send.at[way - 1, k, :, cols], b_rcv.at[way - 1, k, :, cols], dy(way))

    text_grads(2)
    text_grads(1)
    ci_send[...] = jnp.dot(
        slope_s[8 * R:, :], txt_rows, preferred_element_type=F32
    ).astype(BF).reshape(8, R, E)
    ci_copy = copy(ci_send, ci_rcv, other)
    text_grads(3)
    text_grads(0)
    relay_b(2)
    pi_own[...] = jnp.dot(slope_s[:8 * R, :], txt_rows, preferred_element_type=F32).reshape(8, R, E)
    relay_b(1)

    part = jnp.sum(acc)
    lx[0] = jnp.full((8, 128), part, F32)
    lxc = [copy(lx.at[0], lx.at[4 - k], dx(k)) for k in (1, 2, 3)]

    ci_copy.wait_recv()
    pi_own[...] += ci_rcv[...].astype(F32)

    rzp = {}
    rzm = {}

    def send_p(step, q, value):
        zp_send[step, :, parts[q]] = value.astype(BF)
        rzp[step, q] = copy(zp_send.at[step, :, parts[q]], zp_rcv.at[step, :, parts[q]], dz(1))

    def send_m(step, q, value):
        zm_send[step, :, parts[q]] = value.astype(BF)
        rzm[step, q] = copy(zm_send.at[step, :, parts[q]], zm_rcv.at[step, :, parts[q]], dz(7))

    for q in (0, 1):
        send_p(0, q, pi_own[4, :, parts[q]])
        send_m(0, q + 2, pi_own[4, :, parts[q + 2]])
    for q in (0, 1):
        send_p(1, q + 2, pi_own[3, :, parts[q + 2]])
        send_m(1, q, pi_own[5, :, parts[q]])

    def ring(step):
        for q in (0, 1) if step == 1 else (2, 3, 0, 1):
            r = (q + 2) % 4
            rzp[step - 1, q].wait_recv()
            send_p(step, q, pi_own[4 - step, :, parts[q]] + zp_rcv[step - 1, :, parts[q]].astype(F32))
            rzm[step - 1, r].wait_recv()
            send_m(step, r, pi_own[4 + step, :, parts[r]] + zm_rcv[step - 1, :, parts[r]].astype(F32))

    relay_a()
    relay_b(3)
    relay_b(0)
    ring(1)

    def summed(own, *got):
        for part in got:
            own = own + part.astype(F32)
        return own

    for way in (1, 3):
        sa["near", way].wait_recv()
        sa["sum", way].wait_recv()
    a2_send[...] = summed(a_own[1:], a_rcv[0, 1:], a_rcv[2, 1:]).astype(BF)
    a2 = [copy(a2_send.at[k - 1], a2_rcv.at[3 - k], dy(k)) for k in (1, 2, 3)]
    for way in (1, 3):
        for k in (1, 2, 3):
            sb["near", way, k].wait_recv()
            sb["sum", way, k].wait_recv()
    b2_send[...] = summed(b_own[1:], b_rcv[0, 1:], b_rcv[2, 1:]).astype(BF)
    b2 = [copy(b2_send.at[k - 1], b2_rcv.at[3 - k], dx(k)) for k in (1, 2, 3)]
    for way in (1, 3):
        sa["own", way].wait_recv()
        sb["near", way, 0].wait_recv()
        sb["sum", way, 0].wait_recv()
    ga0 = summed(a_own[0], a_rcv[0, 0], a_rcv[2, 0])
    gb0 = summed(b_own[0], b_rcv[0, 0], b_rcv[2, 0])

    for cp in lxc:
        cp.wait_recv()
    ly[0] = (lx[0] + lx[2]) + (lx[1] + lx[3])
    lyc = [copy(ly.at[0], ly.at[4 - k], dy(k)) for k in (1, 2, 3)]

    ring(2)
    ring(3)

    for cp in a2:
        cp.wait_recv()
    for cp in b2:
        cp.wait_recv()
    ga0 = summed(ga0, a2_rcv[0], a2_rcv[1], a2_rcv[2])
    gb0 = summed(gb0, b2_rcv[0], b2_rcv[1], b2_rcv[2])

    def back(m, ga, gb):
        ua = full[m, :, A]
        ub = full[m, :, B]
        inner = jnp.sum(ua * ga, axis=1, keepdims=True) + jnp.sum(ub * gb, axis=1, keepdims=True)
        norm = norms[m, :, 0:1]
        pgf[m, :, A] = ((ga - ua * inner) / norm).astype(BF)
        pgf[m, :, B] = ((gb - ub * inner) / norm).astype(BF)

    def share(m):
        cp = copy(pgf.at[m, :, their_cols], pg64.at[m, mine], fs_partner)
        pg64[m, mine, :] = pgf[m, :, my_cols]
        return cp

    before = len(sent)
    back(1, ga0, gb0)
    pg_txt = share(1)

    def quarter(y_):
        return pl.ds(pl.multiple_of(384 * y_, 128), 384)

    pp = [
        copy(
            pgf.at[1, :, quarter(lax.rem(y + j, 4))],
            pg_plane.at[(4 - i) % 4, (4 - j) % 4], dxy(i, j),
        )
        for i, j in ORDER
    ]
    pg_plane[0, 0] = pgf[1, :, quarter(y)]

    for q in range(4):
        rzp[3, q].wait_recv()
        rzm[3, q].wait_recv()
    gi = pi_own[0] + zp_rcv[3].astype(F32) + zm_rcv[3].astype(F32)
    back(0, gi[:, :H], gi[:, H:])
    pg_img = share(0)

    my_feat = pl.ds(pl.multiple_of(yh * FH, 16), FH)
    their_feat = pl.ds(pl.multiple_of((1 - yh) * FH, 16), FH)

    def feature_terms(m, w, out, into):
        out[...] = dot_nt(pg64[m], w[their_feat, :]).astype(out.dtype)
        return copy(out, into, fs_partner)

    pg_txt.wait_recv()
    fg_txt = feature_terms(1, w_txt, ft_send, ft_rcv)
    for cp in lyc:
        cp.wait_recv()
    lc[0] = (ly[0] + ly[2]) + (ly[1] + ly[3])
    lcc = copy(lc.at[0], lc.at[1], other)
    for cp in fw:
        cp.wait_recv()
    flush(before)
    for cp in pp:
        cp.wait_recv()
    wg[0:512, :] = dot_tn(feat_win[...].reshape(16 * R, 512), pg_plane[...].reshape(16 * R, 384))
    wg[512:528, :] = jnp.zeros((16, 384), F32)
    start = 352 * x - (256 * x + 128 * (x // 2))

    def rows16(k, core):
        first = start + 22 * k + 11 * core
        low = first // 8
        block = wg[pl.ds(pl.multiple_of(low * 8, 8), 24), :]
        return pltpu.roll(block, 24 - (first - low * 8), 0)[:16]

    def cut(k, carry):
        cw_send[k] = rows16(k, 1 - c).astype(BF)
        return carry

    lax.fori_loop(0, 16, cut, 0, unroll=4)
    cw = copy(cw_send, cw_rcv, other)

    lcc.wait_recv()
    lz[0] = lc[0] + lc[1]
    lzc = [copy(lz.at[0], lz.at[8 - k], dz(k)) for k in range(1, 8)]

    cw.wait_recv()

    def add_core(k, carry):
        s2[k] = (rows16(k, c) + cw_rcv[k].astype(F32)).astype(BF)
        return carry

    lax.fori_loop(0, 16, add_core, 0, unroll=4)
    before = len(sent)
    zw = []
    for k in (4, 3, 5, 2, 6, 1, 7, 0):
        zz = lax.rem(z + k, 8)
        zw.append(copy(s2.at[(1 - yl) * 8 + zz], zw_rcv.at[1, (8 - k) % 8], dyz(k)))
        if k:
            zw.append(copy(s2.at[yl * 8 + zz], zw_rcv.at[0, 8 - k], dz(k)))

    pg_img.wait_recv()
    fg_img = feature_terms(0, w_img, fi_send, fi_rcv)
    txt_out[...] = dot_nt(pg64[1], w_txt[my_feat, :])
    img_out[...] = dot_nt(pg64[0], w_img[my_feat, :])

    near = rows16(yl * 8 + z, c) + cw_rcv[yl * 8 + z].astype(F32)
    fg_txt.wait_recv()
    txt_out[...] += ft_rcv[...].astype(F32)
    for cp in lzc:
        cp.wait_recv()
    total = ((lz[0] + lz[4]) + (lz[2] + lz[6])) + ((lz[1] + lz[5]) + (lz[3] + lz[7]))
    loss_out[0] = jnp.max(total) / 8192.0
    flush(before)
    for cp in zw:
        cp.wait_recv()
    far = zw_rcv[1, 0].astype(F32)
    for k in range(1, 8):
        near = near + zw_rcv[0, k].astype(F32)
        far = far + zw_rcv[1, k].astype(F32)
    wg_out[:, pl.ds(pl.multiple_of(384 * yl, 128), 384)] = near[:11, :]
    wg_out[:, pl.ds(pl.multiple_of(384 * (1 - yl), 128), 384)] = far[:11, :]
    fg_img.wait_recv()
    img_out[...] += fi_rcv[...].astype(F32)
    assert counter[0] <= N_SEM
    for cp in sent:
        cp.wait_send()


def hand_out(*refs):
    refs[4][0] = refs[0][0]
    for i in (1, 2, 3):
        refs[4 + i][...] = refs[i][...]


def body(img_feat, txt_feat, img_weight, txt_weight, logit_scale, logit_bias):
    vm = pl.BlockSpec(memory_space=pltpu.VMEM)
    sm = pl.BlockSpec(memory_space=pltpu.SMEM)
    hbm = pl.BlockSpec(memory_space=pltpu.HBM)
    V = pltpu.VMEM
    results = pl.pallas_call(
        kernel,
        out_shape=(
            jax.ShapeDtypeStruct((1,), F32),
            jax.ShapeDtypeStruct((64, FH), F32),
            jax.ShapeDtypeStruct((64, FH), F32),
            jax.ShapeDtypeStruct((11, H), F32),
        ),
        in_specs=[vm, vm, hbm, hbm, hbm, hbm],
        out_specs=(sm, vm, vm, vm),
        scratch_shapes=[
            V((64, FEAT), BF), V((64, FEAT), BF), V((FEAT, H), BF), V((FEAT, H), BF),
            V((2, 64, H), F32), V((2, R, H), F32), V((2, R, E), F32), V((2, R, 128), F32),
            V((4, 4, R, E), BF), V((2, 8, R, E), BF), V((16 * R, 16 * R), BF), V((4, 4, R, 512), BF), V((2, R, FEAT), BF),
            V((2, 4, R, 384), F32), V((2, 4, R, 384), F32),
            V((3, 4, R, H), BF), V((3, 4, R, H), BF), V((4, R, H), F32), V((3, R, H), BF), V((3, R, H), BF),
            V((3, 4, R, H), BF), V((3, 4, R, H), BF), V((4, R, H), F32), V((3, R, H), BF), V((3, R, H), BF),
            V((8, R, E), BF), V((8, R, E), BF), V((8, R, E), F32),
            V((4, R, E), BF), V((4, R, E), BF), V((4, R, E), BF), V((4, R, E), BF),
            V((2, R, E), BF), V((2, 64, H), BF), V((4, 4, R, 384), BF), V((64, FH), BF), V((64, FH), BF), V((64, FH), BF), V((64, FH), BF),
            V((528, 384), F32), V((16, 16, 384), BF), V((16, 16, 384), BF), V((16, 16, 384), BF), V((2, 8, 16, 384), BF),
            V((4, 8, 128), F32), V((4, 8, 128), F32), V((2, 8, 128), F32), V((8, 8, 128), F32),
            V((16 * R, 16 * R), F32),
            pltpu.SemaphoreType.DMA((N_SEM,)),
            pltpu.SemaphoreType.DMA((N_SEM,)),
            pltpu.SemaphoreType.DMA((4,)),
        ],
        compiler_params=pltpu.CompilerParams(
            collective_id=0, has_side_effects=True, vmem_limit_bytes=56 * 1024 * 1024
        ),
        name="fused",
    )(logit_scale.reshape(1, 1), logit_bias.reshape(1, 1), img_feat, txt_feat, img_weight, txt_weight)
    loss, img_grad, txt_grad, w_grad = pl.pallas_call(
        hand_out,
        out_shape=tuple(jax.ShapeDtypeStruct(r.shape, r.dtype) for r in results),
        in_specs=[sm, vm, vm, vm],
        out_specs=(sm, vm, vm, vm),
        name="hand_out",
    )(*results)
    return loss.reshape(()), img_grad, txt_grad, w_grad


def solution(mesh):
    placed = (P("dp", None), P("dp", None), P(None, "fsdp"), P(None, "fsdp"), P(), P())
    return jax.shard_map(
        body,
        mesh=mesh,
        in_specs=placed,
        out_specs=(P(), P("dp", "fsdp"), P("dp", "fsdp"), P("dp", "fsdp")),
        check_vma=False,
    )
```
